256 devices in a mesh: tiles: 64 (over x, z, core), comp: 4 (over y).
Axes of the slice: x: 4, y: 4, z: 8, core: 2. Of those that a mesh axis runs over, the one named last changes fastest.
Arguments:
- action: float32 [768, 32768], P('comp', 'tiles'), may hold values from 0 to 4
- speed_courant: float32 [32], replicated, may hold values from 0.15 to 0.6
- turning: float32 [32768], P('tiles'), may hold values from -0.45 to 0.45
- freq_shift: float32 [32768], P('tiles'), may hold values from -0.45 to 0.45
- wind_speed: float32 [32768], P('tiles'), may hold values from 0.1 to 1.2
- wind_dir: float32 [32768], P('tiles'), may hold values from -3.140625 to 3.140625
- sea_mask: int32 [32768], P('tiles'), may hold values 0 or 1
- neighbours: int32 [4, 32768], P(None, 'tiles'), may hold values from 0 to 768
- halo_rows: int32 [16384], P('tiles'), may hold values from 0 to 511
Outputs:
- updated: float32 [768, 32768], P('comp', 'tiles')
The draws below stay inside these ranges and needn't reach their ends.
All inputs are finite; a program needn't handle non-finite values. No bound on the sum of `sea_mask` on one device may be relied on, other than what follows from the above.
Results may differ from the reference program's by a relative error of at most 0.0003.
Values sent between devices are 32-bit elements; how exact they have to be, the bound alone decides.
A program may use at most 64 MiB of HBM per device.

```python
import math
import jax
import jax.numpy as jnp
from jax import lax

NTH = 24
NK = 32
BLOCK = 128
B_DEV = 4
NSUB = 4
COMPS = 768
PTS_DEV = 512
HALO = 128
SENDS = 16384
POINTS = 32768
N_TILES = 64


def draw_action(key, part):
    key = jax.random.fold_in(key, 11)
    dirs = (jnp.arange(COMPS) // NK).astype(jnp.float32)
    scale = 0.5 + 1.5 * dirs / max(NTH - 1, 1)
    base = jnp.exp(jax.random.uniform(key, (COMPS, POINTS), jnp.float32, math.log(0.05), math.log(2.0)))
    return base * scale[:, None]


def touch_ends(values, rng, least, top_value):
    shape = values.shape
    spot = [jax.random.randint(jax.random.fold_in(rng, axis), (), 0, shape[axis]) for axis in range(len(shape))]
    values = values.at[tuple(spot)].set(least)
    longest = shape.index(max(shape))
    spot[longest] = (spot[longest] + 1) % shape[longest]
    return values.at[tuple(spot)].set(top_value)


def block_scale(rng, shape, pieces, smallest, top_value):
    loudness, own = 1.0, jax.random.fold_in(rng, 6)
    for dim, blocks in pieces:
        draws = jnp.exp(jax.random.uniform(jax.random.fold_in(own, dim), (blocks,), jnp.float32, smallest / len(pieces), top_value / len(pieces)))
        loudness = loudness * jnp.repeat(draws, shape[dim] // blocks).reshape([-1 if axis == dim else 1 for axis in range(len(shape))])
    return loudness


def setup_inputs(seed: int = 0) -> dict:
    splits = jax.random.split(jax.random.key(seed), 10)
    return {
        "action": draw_action(jax.random.fold_in(splits[9], 71), 0),
        "speed_courant": jnp.clip(jax.random.uniform(splits[1], (NK,), jnp.float32, 0.15, 0.6), 0.15, 0.6),
        "turning": jnp.clip(jax.random.uniform(splits[2], (POINTS,), jnp.float32, -0.45, 0.45) * block_scale(splits[2], (POINTS,), ((0, 64),), -0.4, 0.0), -0.45, 0.45),
        "freq_shift": jnp.clip(jax.random.uniform(splits[3], (POINTS,), jnp.float32, -0.45, 0.45) * block_scale(splits[3], (POINTS,), ((0, 64),), -0.4, 0.0), -0.45, 0.45),
        "wind_speed": jnp.clip(0.1 + 1.1 * jax.random.uniform(splits[4], (POINTS,), jnp.float32) ** block_scale(splits[4], (POINTS,), ((0, 64),), -0.2, 0.2), 0.1, 1.2),
        "wind_dir": jnp.clip(jax.random.uniform(splits[5], (POINTS,), jnp.float32, -3.140625, 3.140625), -3.140625, 3.140625),
        "sea_mask": touch_ends((jax.random.randint(splits[6], (POINTS,), 0, 10) < 9).astype(jnp.int32), jax.random.fold_in(splits[6], 1), 0, 1),
        "neighbours": touch_ends(jax.random.randint(splits[7], (4, POINTS), 0, PTS_DEV + 2 * HALO + 1), jax.random.fold_in(splits[7], 1), 0, PTS_DEV + 2 * HALO).astype(jnp.int32),
        "halo_rows": touch_ends(jax.random.randint(splits[8], (SENDS,), 0, PTS_DEV), jax.random.fold_in(splits[8], 1), 0, PTS_DEV - 1).astype(jnp.int32),
    }


def sigma_table(freqs):
    offsets = (jnp.arange(freqs) - freqs // 2).astype(jnp.float32)
    return jnp.exp(offsets * jnp.float32(math.log(1.1)))


def angle_table(count, total):
    return jnp.arange(count).astype(jnp.float32) * jnp.float32(2.0 * math.pi / total)


def advect(spectrum, left_rim, right_rim, links, wet_points, speed_x, speed_y):
    empty_slot = jnp.zeros(spectrum.shape[:2] + (1,), jnp.float32)
    extended = jnp.concatenate([left_rim, spectrum, right_rim, empty_slot], axis=2)
    from_west = jnp.take(extended, links[0], axis=2)
    from_east = jnp.take(extended, links[1], axis=2)
    from_south = jnp.take(extended, links[2], axis=2)
    from_north = jnp.take(extended, links[3], axis=2)
    upwind_x = jnp.where(speed_x > 0, from_west, from_east)
    upwind_y = jnp.where(speed_y > 0, from_south, from_north)
    return wet_points * (spectrum - jnp.abs(speed_x) * (spectrum - upwind_x) - jnp.abs(speed_y) * (spectrum - upwind_y))


def refract(spectrum, before, beyond, turning):
    rate = turning[None, None, :]
    return spectrum - jnp.abs(rate) * (spectrum - jnp.where(rate > 0, before, beyond))


def shift_freq(spectrum, shifting):
    empty_row = jnp.zeros_like(spectrum[:, :1])
    lower_freq = jnp.concatenate([empty_row, spectrum[:, :-1]], axis=1)
    upper_freq = jnp.concatenate([spectrum[:, 1:], empty_row], axis=1)
    rate = shifting[None, None, :]
    return spectrum - jnp.abs(rate) * (spectrum - jnp.where(rate > 0, lower_freq, upper_freq))


def apply_sources(shifted, energy, moment, angles, sigmas, speed, direction, wet_points):
    mean_freq = moment / jnp.maximum(energy, 0.05)
    sigcol = sigmas[None, :, None]
    damping = 0.005 * (sigcol * sigcol) * (mean_freq * mean_freq * mean_freq * energy * energy)[None, None, :]
    aligned = jnp.cos(angles[:, None, None] - direction[None, None, :])
    growth = 0.4 * jnp.maximum(speed[None, None, :] * sigcol * aligned - 0.3, 0.0)
    return wet_points * shifted * (1.0 + growth) / (1.0 + damping)


def sources(spectrum, turning, shifting, speed, direction, wet_points, angles, sigmas, comps):
    before = jnp.roll(spectrum, 1, axis=0)
    beyond = jnp.roll(spectrum, -1, axis=0)
    refracted = refract(spectrum, before, beyond, turning)
    shifted = shift_freq(refracted, shifting)
    energy = jnp.sum(shifted * sigmas[None, :, None], axis=(0, 1)) / comps
    moment = jnp.sum(shifted * (sigmas * sigmas)[None, :, None], axis=(0, 1)) / comps
    return apply_sources(shifted, energy, moment, angles, sigmas, speed, direction, wet_points)


def pick_rows(spectrum, rows):
    return jnp.take(spectrum, rows, axis=2)


def reference(action, speed_courant, turning, freq_shift, wind_speed, wind_dir, sea_mask, neighbours, halo_rows):
    tiles_count = N_TILES
    points = B_DEV * BLOCK
    width = HALO
    wet = sea_mask.astype(jnp.float32).reshape(tiles_count, points)
    spectrum = action.reshape(NTH, NK, tiles_count, points).transpose(2, 0, 1, 3) * wet[:, None, None, :]
    angles = angle_table(NTH, NTH)
    sigmas = sigma_table(NK)
    speed_x = (speed_courant[None, :] * jnp.cos(angles)[:, None])[:, :, None]
    speed_y = (speed_courant[None, :] * jnp.sin(angles)[:, None])[:, :, None]
    send_rows = halo_rows.reshape(tiles_count, 2 * width)
    links = neighbours.reshape(4, tiles_count, points).transpose(1, 0, 2)

    def one_tile(packed):
        return advect(packed[0], packed[1], packed[2], packed[3], packed[4], speed_x, speed_y)

    for substep in range(NSUB):
        outgoing = jax.vmap(pick_rows)(spectrum, send_rows)
        nothing = jnp.zeros_like(outgoing[:1, :, :, :width])
        left_rim = jnp.concatenate([nothing, outgoing[:-1, :, :, width:]], axis=0)
        right_rim = jnp.concatenate([outgoing[1:, :, :, :width], nothing], axis=0)
        spectrum = lax.map(one_tile, (spectrum, left_rim, right_rim, links, wet))

    def tile_sources(packed):
        return sources(packed[0], packed[1], packed[2], packed[3], packed[4], packed[5], angles, sigmas, COMPS)

    result = lax.map(tile_sources, (spectrum, turning.reshape(tiles_count, points), freq_shift.reshape(tiles_count, points), wind_speed.reshape(tiles_count, points), wind_dir.reshape(tiles_count, points), wet))
    return result.transpose(1, 2, 0, 3).reshape(COMPS, POINTS)
```

```python
import math

import jax
import jax.numpy as jnp
import numpy as np
from jax import lax
from jax.experimental import pallas as pl
from jax.experimental.pallas import tpu as pltpu
from jax.sharding import PartitionSpec as P

NSUB = 4
NTH = 24
NK = 32
PTS = 512
RIM = 128
EXT = PTS + 2 * RIM
COMP_AXIS = 4
DIRS = NTH // COMP_AXIS
ROWS = DIRS * NK
COMPS = NTH * NK
OWN_N = 2 * PTS
SEND_N = 4 * RIM
GROUPS = ((0, 3), (3, 6))
MESH = pl.DeviceIdType.MESH
STEP = np.float32(2.0 * math.pi / NTH)
LOG_RATIO = np.float32(math.log(1.1))


def pick(index, values):
    chosen = jnp.float32(values[0])
    for place in range(1, len(values)):
        chosen = jnp.where(index == place, jnp.float32(values[place]), chosen)
    return chosen


def halves(values):
    high = values.astype(jnp.bfloat16)
    low = (values - high.astype(jnp.float32)).astype(jnp.bfloat16)
    return jnp.concatenate([high, low], axis=0)


def gathered(split, table):
    both = jnp.dot(split, table, preferred_element_type=jnp.float32)
    rows = both.shape[0] // 2
    return both[:rows] + both[rows:]


def wide(column, lanes):
    return jnp.concatenate([column] * (lanes // RIM), axis=1)


def onehot(first, count, index):
    places = lax.broadcasted_iota(jnp.int32, (count, index.shape[1]), 0) + first
    return jnp.where(places == index, 1.0, 0.0).astype(jnp.bfloat16)


def kernel(
    action_hbm,
    speed_hbm,
    turning_hbm,
    shift_hbm,
    wind_hbm,
    dir_hbm,
    mask_hbm,
    links_hbm,
    rows_hbm,
    out_ref,
    spec,
    speed,
    turning,
    shift,
    wind,
    wdir,
    mask,
    links,
    rows,
    table,
    send_table,
    across,
    along,
    keep,
    outgoing,
    rim,
    pending,
    pending_send,
    gain,
    ghost,
    part,
    parts,
    load_sem,
    halo_send,
    halo_recv,
    ghost_send,
    ghost_recv,
    part_send,
    part_recv,
):
    tile = lax.axis_index("tiles")
    comp = lax.axis_index("comp")
    tiles = lax.axis_size("tiles")
    before_tile = lax.rem(tile + tiles - 1, tiles)
    after_tile = lax.rem(tile + 1, tiles)
    comp_at = [lax.rem(comp + step, COMP_AXIS) for step in range(COMP_AXIS)]

    barrier = pltpu.get_barrier_semaphore()
    for place in (
        (before_tile, comp),
        (after_tile, comp),
        (tile, comp_at[1]),
        (tile, comp_at[2]),
        (tile, comp_at[3]),
    ):
        pl.semaphore_signal(barrier, inc=1, device_id=place, device_id_type=MESH)

    loads = [
        pltpu.make_async_copy(source, target, load_sem.at[number])
        for number, (source, target) in enumerate(
            (
                (rows_hbm, rows),
                (mask_hbm, mask),
                (action_hbm, spec),
                (links_hbm, links),
                (speed_hbm, speed),
                (turning_hbm, turning),
                (shift_hbm, shift),
                (wind_hbm, wind),
                (dir_hbm, wdir),
            )
        )
    ]
    for load in loads:
        load.start()

    def halo_copies(step, group):
        first, last = (GROUPS[group][0] * NK, GROUPS[group][1] * NK)
        span = pl.ds(first, last - first)
        copies = []
        for side, target in ((0, before_tile), (1, after_tile)):
            copies.append(
                pltpu.make_async_remote_copy(
                    src_ref=outgoing.at[step, side, span],
                    dst_ref=rim.at[step, 1 - side, span],
                    send_sem=halo_send.at[step, group, side],
                    recv_sem=halo_recv.at[step, group, 1 - side],
                    device_id=(target, comp),
                    device_id_type=MESH,
                )
            )
        return copies

    started = []

    def send_halo(step, group, values):
        first, last = (GROUPS[group][0] * NK, GROUPS[group][1] * NK)
        outgoing[step, 0, first:last] = values[:, :RIM]
        outgoing[step, 1, first:last] = values[:, RIM:]
        for copy in halo_copies(step, group):
            copy.start()
            started.append(copy)

    loads[0].wait()
    send_table[...] = onehot(0, PTS, rows[...])
    loads[1].wait()
    wet = mask[...].astype(jnp.float32)
    loads[2].wait()
    spec[...] = spec[...] * wet
    splits = []
    first_sends = []
    for first, last in GROUPS:
        split = halves(spec[first * NK : last * NK])
        splits.append(split)
        first_sends.append(gathered(split, send_table[...]))
    pl.semaphore_wait(barrier, 5)
    for group in range(len(GROUPS)):
        send_halo(0, group, first_sends[group])

    loads[4].wait()
    diagonal = lax.broadcasted_iota(jnp.int32, (NK, NK), 0) == lax.broadcasted_iota(
        jnp.int32, (NK, NK), 1
    )
    courant = jnp.sum(jnp.where(diagonal, speed[...], 0.0), axis=1, keepdims=True)
    courant = jnp.broadcast_to(courant, (NK, RIM))
    angles = np.arange(NTH).astype(np.float32) * STEP
    cosines = np.abs(np.cos(angles)).reshape(COMP_AXIS, DIRS)
    sines = np.abs(np.sin(angles)).reshape(COMP_AXIS, DIRS)
    for d in range(DIRS):
        span = slice(d * NK, (d + 1) * NK)
        speed_x = courant * pick(comp, cosines[:, d])
        speed_y = courant * pick(comp, sines[:, d])
        across[span] = speed_x
        along[span] = speed_y
        keep[span] = 1.0 - speed_x - speed_y

    loads[3].wait()
    west_side = jnp.logical_or(comp == 0, comp == COMP_AXIS - 1)
    south_side = comp < 2
    for axis, index in enumerate(
        (
            jnp.where(west_side, links[0:1], links[1:2]),
            jnp.where(south_side, links[2:3], links[3:4]),
        )
    ):
        no_left = jnp.logical_and(tile == 0, index < RIM)
        no_right = jnp.logical_and(tile == tiles - 1, index >= RIM + PTS)
        nothing = jnp.logical_or(jnp.logical_or(no_left, no_right), mask[...] == 0)
        index = jnp.where(nothing, EXT, index)
        lanes = pl.ds(axis * PTS, PTS)
        table[0:PTS, lanes] = onehot(RIM, PTS, index)
        table[PTS : PTS + RIM, lanes] = onehot(0, RIM, index)
        table[PTS + RIM : EXT, lanes] = onehot(RIM + PTS, RIM, index)
    for axis in range(2):
        picked = jnp.dot(
            table[:, axis * PTS : (axis + 1) * PTS],
            send_table[...],
            preferred_element_type=jnp.float32,
        )
        first = OWN_N + axis * 2 * RIM
        table[:, first : first + 2 * RIM] = picked.astype(jnp.bfloat16)

    def own_part(group, split, values, sends, with_sends):
        first, last = (GROUPS[group][0] * NK, GROUPS[group][1] * NK)
        span = slice(first, last)
        picked = gathered(split, table[0:PTS, 0:OWN_N])
        pending[span] = (
            wide(keep[span], PTS) * values
            + wide(across[span], PTS) * picked[:, :PTS]
            + wide(along[span], PTS) * picked[:, PTS:]
        )
        if with_sends:
            picked = gathered(split, table[0:PTS, OWN_N:])
            pending_send[span] = (
                wide(keep[span], 2 * RIM) * sends
                + wide(across[span], 2 * RIM) * picked[:, : 2 * RIM]
                + wide(along[span], 2 * RIM) * picked[:, 2 * RIM :]
            )

    for group, (first, last) in enumerate(GROUPS):
        own_part(group, splits[group], spec[first * NK : last * NK], first_sends[group], True)

    for number in (5, 6, 7, 8):
        loads[number].wait()
    sigma = jnp.exp(
        (lax.broadcasted_iota(jnp.int32, (NK, RIM), 0) - NK // 2).astype(jnp.float32) * LOG_RATIO
    )
    sigma = wide(sigma, PTS)
    angle = (lax.broadcasted_iota(jnp.int32, (8, PTS), 0) + comp * DIRS).astype(jnp.float32) * STEP
    aligned = jnp.cos(angle - wdir[...])
    driven = wind[...] * sigma
    for d in range(DIRS):
        grown = 0.4 * jnp.maximum(driven * aligned[d : d + 1] - 0.3, 0.0)
        gain[d * NK : (d + 1) * NK] = wet * (1.0 + grown)

    ghost_copies = [
        pltpu.make_async_remote_copy(
            src_ref=spec.at[pl.ds(at * NK, NK)],
            dst_ref=ghost.at[slot],
            send_sem=ghost_send.at[slot],
            recv_sem=ghost_recv.at[slot],
            device_id=(tile, target),
            device_id_type=MESH,
        )
        for slot, at, target in ((0, DIRS - 1, comp_at[1]), (1, 0, comp_at[3]))
    ]

    for step in range(NSUB):
        for group, (low, high) in enumerate(GROUPS):
            first, last = (low * NK, high * NK)
            span = slice(first, last)
            for copy in halo_copies(step, group):
                copy.wait_recv()
            split = halves(jnp.concatenate([rim[step, 0, span], rim[step, 1, span]], axis=1))
            if step < NSUB - 1:
                picked = gathered(split, table[PTS:EXT, OWN_N:])
                sends = (
                    pending_send[span]
                    + wide(across[span], 2 * RIM) * picked[:, : 2 * RIM]
                    + wide(along[span], 2 * RIM) * picked[:, 2 * RIM :]
                )
                send_halo(step + 1, group, sends)
            picked = gathered(split, table[PTS:EXT, 0:OWN_N])
            values = (
                pending[span]
                + wide(across[span], PTS) * picked[:, :PTS]
                + wide(along[span], PTS) * picked[:, PTS:]
            )
            if step < NSUB - 1:
                own_part(group, halves(values), values, sends, step < NSUB - 2)
            else:
                spec[span] = values
                if low == 0:
                    ghost_copies[1].start()
                if high == DIRS:
                    ghost_copies[0].start()

    turn = turning[...]
    moved = shift[...]
    freq = lax.broadcasted_iota(jnp.int32, (NK, PTS), 0)

    def shifted(values):
        lower = jnp.where(freq == 0, 0.0, pltpu.roll(values, 1, 0))
        upper = jnp.where(freq == NK - 1, 0.0, pltpu.roll(values, NK - 1, 0))
        return values - jnp.abs(moved) * (values - jnp.where(moved > 0, lower, upper))

    total = spec[0:NK]
    for d in range(1, DIRS):
        total = total + spec[d * NK : (d + 1) * NK]
    total = shifted(total) * sigma
    energy = jnp.sum(total, axis=0, keepdims=True)
    moment = jnp.sum(total * sigma, axis=0, keepdims=True)
    part[0:1] = energy
    part[1:2] = moment
    part_copies = [
        pltpu.make_async_remote_copy(
            src_ref=part,
            dst_ref=parts.at[hop - 1],
            send_sem=part_send.at[hop - 1],
            recv_sem=part_recv.at[hop - 1],
            device_id=(tile, comp_at[hop]),
            device_id_type=MESH,
        )
        for hop in (2, 1, 3)
    ]
    for copy in part_copies:
        copy.start()

    def refracted(d):
        values = spec[d * NK : (d + 1) * NK]
        before = ghost[0] if d == 0 else spec[(d - 1) * NK : d * NK]
        beyond = ghost[1] if d == DIRS - 1 else spec[(d + 1) * NK : (d + 2) * NK]
        return values - jnp.abs(turn) * (values - jnp.where(turn > 0, before, beyond))

    def grow(d):
        span = slice(d * NK, (d + 1) * NK)
        gain[span] = gain[span] * shifted(refracted(d))

    for d in range(1, DIRS - 1):
        grow(d)
    ghost_copies[0].wait_recv()
    grow(0)
    ghost_copies[1].wait_recv()
    grow(DIRS - 1)
    for copy in part_copies:
        copy.wait_recv()
    whole = (part[...] + parts[0] + parts[1] + parts[2]) * jnp.float32(1.0 / COMPS)
    energy = whole[0:1]
    mean_freq = whole[1:2] / jnp.maximum(energy, 0.05)
    strength = mean_freq * mean_freq * mean_freq * energy * energy
    damping = 0.005 * (sigma * sigma) * strength
    factor = 1.0 / (1.0 + damping)
    for d in range(DIRS):
        span = slice(d * NK, (d + 1) * NK)
        out_ref[span] = gain[span] * factor

    for copy in started + ghost_copies + part_copies:
        copy.wait_send()


def shards(
    action,
    speed_courant,
    turning,
    freq_shift,
    wind_speed,
    wind_dir,
    sea_mask,
    neighbours,
    halo_rows,
):
    vmem = pltpu.VMEM
    f32 = jnp.float32
    dma = pltpu.SemaphoreType.DMA
    groups = len(GROUPS)

    def row(values):
        return values.reshape(1, values.shape[0])

    return pl.pallas_call(
        kernel,
        out_shape=jax.ShapeDtypeStruct((ROWS, PTS), f32),
        in_specs=[pl.BlockSpec(memory_space=pl.ANY)] * 9,
        out_specs=pl.BlockSpec(memory_space=pltpu.VMEM),
        scratch_shapes=[
            vmem((ROWS, PTS), f32),
            vmem((1, NK), f32),
            vmem((1, PTS), f32),
            vmem((1, PTS), f32),
            vmem((1, PTS), f32),
            vmem((1, PTS), f32),
            vmem((1, PTS), jnp.int32),
            vmem((4, PTS), jnp.int32),
            vmem((1, 2 * RIM), jnp.int32),
            vmem((EXT, OWN_N + SEND_N), jnp.bfloat16),
            vmem((PTS, 2 * RIM), jnp.bfloat16),
            vmem((ROWS, RIM), f32),
            vmem((ROWS, RIM), f32),
            vmem((ROWS, RIM), f32),
            vmem((NSUB, 2, ROWS, RIM), f32),
            vmem((NSUB, 2, ROWS, RIM), f32),
            vmem((ROWS, PTS), f32),
            vmem((ROWS, 2 * RIM), f32),
            vmem((ROWS, PTS), f32),
            vmem((2, NK, PTS), f32),
            vmem((2, PTS), f32),
            vmem((3, 2, PTS), f32),
            dma((9,)),
            dma((NSUB, groups, 2)),
            dma((NSUB, groups, 2)),
            dma((2,)),
            dma((2,)),
            dma((3,)),
            dma((3,)),
        ],
        compiler_params=pltpu.CompilerParams(
            collective_id=0, has_side_effects=True, vmem_limit_bytes=48 * 1024 * 1024
        ),
        name="wave_step",
    )(
        action,
        row(speed_courant),
        row(turning),
        row(freq_shift),
        row(wind_speed),
        row(wind_dir),
        row(sea_mask),
        neighbours,
        row(halo_rows),
    )


def solution(mesh):
    placed = (
        P("comp", "tiles"),
        P(),
        P("tiles"),
        P("tiles"),
        P("tiles"),
        P("tiles"),
        P("tiles"),
        P(None, "tiles"),
        P("tiles"),
    )
    return jax.shard_map(
        shards, mesh=mesh, in_specs=placed, out_specs=P("comp", "tiles"), check_vma=False
    )
```

```python
import math

import jax
import jax.numpy as jnp
import numpy as np
from jax import lax
from jax.experimental import pallas as pl
from jax.experimental.pallas import tpu as pltpu
from jax.sharding import PartitionSpec as P

NSUB = 4
NTH = 24
NK = 32
PTS = 512
RIM = 128
EXT = PTS + 2 * RIM
COMP_AXIS = 4
DIRS = NTH // COMP_AXIS
ROWS = DIRS * NK
COMPS = NTH * NK
OWN_N = 2 * PTS
SEND_N = 4 * RIM
NEAR, FAR = 0, 1
GROUPS = ((0, 3), (3, 6))
MESH = pl.DeviceIdType.MESH
STEP = np.float32(2.0 * math.pi / NTH)
LOG_RATIO = np.float32(math.log(1.1))


def pick(index, values):
    chosen = jnp.float32(values[0])
    for place in range(1, len(values)):
        chosen = jnp.where(index == place, jnp.float32(values[place]), chosen)
    return chosen


def halves(values):
    high = values.astype(jnp.bfloat16)
    low = (values - high.astype(jnp.float32)).astype(jnp.bfloat16)
    return jnp.concatenate([high, low], axis=0)


def gathered(split, table):
    both = jnp.dot(split, table, preferred_element_type=jnp.float32)
    rows = both.shape[0] // 2
    return both[:rows] + both[rows:]


def wide(column, lanes):
    return jnp.concatenate([column] * (lanes // RIM), axis=1)


def onehot(first, count, index):
    places = lax.broadcasted_iota(jnp.int32, (count, index.shape[1]), 0) + first
    return jnp.where(places == index, 1.0, 0.0).astype(jnp.bfloat16)


def kernel(
    action_hbm,
    speed_hbm,
    turning_hbm,
    shift_hbm,
    wind_hbm,
    dir_hbm,
    mask_hbm,
    links_hbm,
    rows_hbm,
    out_ref,
    spec,
    speed,
    turning,
    shift,
    wind,
    wdir,
    mask,
    links,
    rows,
    table,
    send_table,
    far_table,
    across,
    along,
    keep,
    outgoing,
    rim,
    pending,
    pending_send,
    mended,
    gain,
    ghost,
    part,
    parts,
    spots,
    far_spots,
    load_sem,
    halo_send,
    halo_recv,
    ghost_send,
    ghost_recv,
    part_send,
    part_recv,
    spot_send,
    spot_recv,
):
    tile = lax.axis_index("tiles")
    comp = lax.axis_index("comp")
    tiles = lax.axis_size("tiles")
    first_core = lax.rem(tile, 2) == 0
    near_tile = jnp.where(first_core, tile + 1, tile - 1)
    far_tile = jnp.where(first_core, tile - 1, tile + 1)
    has_far = jnp.logical_and(far_tile >= 0, far_tile < tiles)
    far_tile = jnp.clip(far_tile, 0, tiles - 1)
    comp_at = [lax.rem(comp + step, COMP_AXIS) for step in range(COMP_AXIS)]

    barrier = pltpu.get_barrier_semaphore()
    for place in (
        (near_tile, comp),
        (tile, comp_at[1]),
        (tile, comp_at[2]),
        (tile, comp_at[3]),
    ):
        pl.semaphore_signal(barrier, inc=1, device_id=place, device_id_type=MESH)

    @pl.when(has_far)
    def _():
        pl.semaphore_signal(barrier, inc=1, device_id=(far_tile, comp), device_id_type=MESH)

    loads = [
        pltpu.make_async_copy(source, target, load_sem.at[number])
        for number, (source, target) in enumerate(
            (
                (rows_hbm, rows),
                (mask_hbm, mask),
                (action_hbm, spec),
                (links_hbm, links),
                (speed_hbm, speed),
                (turning_hbm, turning),
                (shift_hbm, shift),
                (wind_hbm, wind),
                (dir_hbm, wdir),
            )
        )
    ]
    for load in loads:
        load.start()

    def span_of(group):
        return slice(GROUPS[group][0] * NK, GROUPS[group][1] * NK)

    def halo_copy(level, side, group):
        first, last = (GROUPS[group][0] * NK, GROUPS[group][1] * NK)
        span = pl.ds(first, last - first)
        return pltpu.make_async_remote_copy(
            src_ref=outgoing.at[level, side, span],
            dst_ref=rim.at[level, side, span],
            send_sem=halo_send.at[level, side, group],
            recv_sem=halo_recv.at[level, side, group],
            device_id=(near_tile if side == NEAR else far_tile, comp),
            device_id_type=MESH,
        )

    def only_if_far(side, action):
        if side == NEAR:
            action()
        else:
            pl.when(has_far)(action)

    def send_halo(level, side, group, values):
        outgoing[level, side, span_of(group)] = values
        only_if_far(side, lambda: halo_copy(level, side, group).start())

    def await_halo(level, side, group):
        only_if_far(side, lambda: halo_copy(level, side, group).wait_recv())

    loads[0].wait()
    low_rows, high_rows = (rows[:, 0:RIM], rows[:, RIM : 2 * RIM])
    near_rows = jnp.where(first_core, high_rows, low_rows)
    far_rows = jnp.where(first_core, low_rows, high_rows)
    picker = onehot(0, PTS, jnp.concatenate([near_rows, far_rows], axis=1))
    loads[1].wait()
    wet = mask[...].astype(jnp.float32)
    loads[2].wait()
    spec[...] = spec[...] * wet
    splits = []
    first_sends = []
    for group in range(len(GROUPS)):
        split = halves(spec[span_of(group)])
        splits.append(split)
        first_sends.append(gathered(split, picker))

    @pl.when(jnp.logical_not(has_far))
    def _():
        for level in range(NSUB):
            rim[level, FAR] = jnp.zeros((ROWS, RIM), jnp.float32)
        far_spots[...] = jnp.full((1, 2 * RIM), float(RIM), jnp.float32)

    pl.semaphore_wait(barrier, jnp.where(has_far, 5, 4))

    for group in range(len(GROUPS)):
        send_halo(0, FAR, group, first_sends[group][:, RIM:])
        send_halo(0, NEAR, group, first_sends[group][:, :RIM])

    loads[3].wait()
    west_side = jnp.logical_or(comp == 0, comp == COMP_AXIS - 1)
    south_side = comp < 2
    near_first = jnp.where(first_core, RIM + PTS, 0)
    far_first = jnp.where(first_core, 0, RIM + PTS)
    for axis, index in enumerate(
        (
            jnp.where(west_side, links[0:1], links[1:2]),
            jnp.where(south_side, links[2:3], links[3:4]),
        )
    ):
        no_left = jnp.logical_and(tile == 0, index < RIM)
        no_right = jnp.logical_and(tile == tiles - 1, index >= RIM + PTS)
        nothing = jnp.logical_or(jnp.logical_or(no_left, no_right), mask[...] == 0)
        index = jnp.where(nothing, EXT, index)
        lanes = pl.ds(axis * PTS, PTS)
        table[0:PTS, lanes] = onehot(RIM, PTS, index)
        table[PTS : PTS + RIM, lanes] = onehot(near_first, RIM, index)
        table[PTS + RIM : EXT, lanes] = onehot(far_first, RIM, index)
    counted = lax.broadcasted_iota(jnp.int32, (RIM, RIM), 0).astype(jnp.float32)
    for axis in range(2):
        picked = jnp.dot(
            table[:, axis * PTS : (axis + 1) * PTS], picker, preferred_element_type=jnp.float32
        )
        for side in (NEAR, FAR):
            lanes = slice(RIM * (2 * side + axis), RIM * (2 * side + axis + 1))
            chosen = picked[:, side * RIM : (side + 1) * RIM]
            send_table[:, lanes] = chosen.astype(jnp.bfloat16)
        block = picked[PTS + RIM : EXT, RIM : 2 * RIM]
        spots[:, axis * RIM : (axis + 1) * RIM] = float(RIM) + jnp.sum(
            block * (counted - float(RIM)), axis=0, keepdims=True
        )
    spot_copy = pltpu.make_async_remote_copy(
        src_ref=spots,
        dst_ref=far_spots,
        send_sem=spot_send,
        recv_sem=spot_recv,
        device_id=(far_tile, comp),
        device_id_type=MESH,
    )
    pl.when(has_far)(lambda: spot_copy.start())

    loads[4].wait()
    diagonal = lax.broadcasted_iota(jnp.int32, (NK, NK), 0) == lax.broadcasted_iota(
        jnp.int32, (NK, NK), 1
    )
    courant = jnp.sum(jnp.where(diagonal, speed[...], 0.0), axis=1, keepdims=True)
    courant = jnp.broadcast_to(courant, (NK, RIM))
    angles = np.arange(NTH).astype(np.float32) * STEP
    cosines = np.abs(np.cos(angles)).reshape(COMP_AXIS, DIRS)
    sines = np.abs(np.sin(angles)).reshape(COMP_AXIS, DIRS)
    for d in range(DIRS):
        span = slice(d * NK, (d + 1) * NK)
        speed_x = courant * pick(comp, cosines[:, d])
        speed_y = courant * pick(comp, sines[:, d])
        across[span] = speed_x
        along[span] = speed_y
        keep[span] = 1.0 - speed_x - speed_y

    def weighed(group, picked):
        span = span_of(group)
        lanes = picked.shape[1] // 2
        return (
            wide(across[span], lanes) * picked[:, :lanes]
            + wide(along[span], lanes) * picked[:, lanes:]
        )

    def from_points(group, split, places):
        return weighed(group, gathered(split, table[places, :]))

    def from_sends(group, split, places, side):
        lanes = slice(2 * RIM * side, 2 * RIM * (side + 1))
        return weighed(group, gathered(split, send_table[places, lanes]))

    OWN, NEAR_ROWS, FAR_ROWS, RIMS = (
        slice(0, PTS),
        slice(PTS, PTS + RIM),
        slice(PTS + RIM, EXT),
        slice(PTS, EXT),
    )

    def own_part(group, values, sends):
        span = span_of(group)
        split = halves(values)
        pending[span] = wide(keep[span], PTS) * values + from_points(group, split, OWN)
        if sends is not None:
            for side in (NEAR, FAR):
                pending_send[side, span] = keep[span] * sends[side] + from_sends(
                    group, split, OWN, side
                )

    for group in range(len(GROUPS)):
        sends = first_sends[group]
        own_part(group, spec[span_of(group)], (sends[:, :RIM], sends[:, RIM:]))

    for number in (5, 6, 7, 8):
        loads[number].wait()
    sigma = jnp.exp(
        (lax.broadcasted_iota(jnp.int32, (NK, RIM), 0) - NK // 2).astype(jnp.float32) * LOG_RATIO
    )
    sigma = wide(sigma, PTS)
    angle = (lax.broadcasted_iota(jnp.int32, (8, PTS), 0) + comp * DIRS).astype(jnp.float32) * STEP
    aligned = jnp.cos(angle - wdir[...])
    driven = wind[...] * sigma

    def wind_part():
        for d in range(DIRS):
            grown = 0.4 * jnp.maximum(driven * aligned[d : d + 1] - 0.3, 0.0)
            gain[d * NK : (d + 1) * NK] = wet * (1.0 + grown)

    ghost_copies = [
        pltpu.make_async_remote_copy(
            src_ref=spec.at[pl.ds(at * NK, NK)],
            dst_ref=ghost.at[slot],
            send_sem=ghost_send.at[slot],
            recv_sem=ghost_recv.at[slot],
            device_id=(tile, target),
            device_id_type=MESH,
        )
        for slot, at, target in ((0, DIRS - 1, comp_at[1]), (1, 0, comp_at[3]))
    ]

    for level in range(0, NSUB, 2):
        more = level + 2 < NSUB
        for group in range(len(GROUPS)):
            span = span_of(group)
            await_halo(level, NEAR, group)
            split = halves(rim[level, NEAR, span])
            sends = pending_send[FAR, span] + from_sends(group, split, NEAR_ROWS, FAR)
            send_halo(level + 1, FAR, group, sends)
            pending_send[NEAR, span] = pending_send[NEAR, span] + from_sends(
                group, split, NEAR_ROWS, NEAR
            )
            pending[span] = pending[span] + from_points(group, split, NEAR_ROWS)
        if level == 0:
            wind_part()
            pl.when(has_far)(lambda: spot_copy.wait_recv())
            places = lax.broadcasted_iota(jnp.int32, (RIM, 2 * RIM), 0).astype(jnp.float32)
            far_table[...] = jnp.where(places == far_spots[...], 1.0, 0.0).astype(jnp.bfloat16)
        for group in range(len(GROUPS)):
            span = span_of(group)
            mended[span] = weighed(
                group, gathered(halves(outgoing[level, FAR, span]), far_table[...])
            )
        for group in range(len(GROUPS)):
            span = span_of(group)
            await_halo(level, FAR, group)
            split = halves(rim[level, FAR, span])
            near = pending_send[NEAR, span] + from_sends(group, split, FAR_ROWS, NEAR)
            send_halo(level + 1, NEAR, group, near)
            far = None
            if more:
                far = outgoing[level + 1, FAR, span] + from_sends(group, split, FAR_ROWS, FAR)
            values = pending[span] + from_points(group, split, FAR_ROWS)
            own_part(group, values, (near, far) if more else None)
        for group, (low, high) in enumerate(GROUPS):
            span = span_of(group)
            await_halo(level + 1, FAR, group)
            far_rim = rim[level + 1, FAR, span] + mended[span]
            await_halo(level + 1, NEAR, group)
            split = halves(jnp.concatenate([rim[level + 1, NEAR, span], far_rim], axis=1))
            if more:
                sends = []
                for side in (FAR, NEAR):
                    values = pending_send[side, span] + from_sends(group, split, RIMS, side)
                    send_halo(level + 2, side, group, values)
                    sends.append(values)
            values = pending[span] + from_points(group, split, RIMS)
            if more:
                own_part(group, values, (sends[1], sends[0]))
            else:
                spec[span] = values
                if low == 0:
                    ghost_copies[1].start()
                if high == DIRS:
                    ghost_copies[0].start()

    turn = turning[...]
    moved = shift[...]
    freq = lax.broadcasted_iota(jnp.int32, (NK, PTS), 0)

    def shifted(values):
        lower = jnp.where(freq == 0, 0.0, pltpu.roll(values, 1, 0))
        upper = jnp.where(freq == NK - 1, 0.0, pltpu.roll(values, NK - 1, 0))
        return values - jnp.abs(moved) * (values - jnp.where(moved > 0, lower, upper))

    total = spec[0:NK]
    for d in range(1, DIRS):
        total = total + spec[d * NK : (d + 1) * NK]
    total = shifted(total) * sigma
    energy = jnp.sum(total, axis=0, keepdims=True)
    moment = jnp.sum(total * sigma, axis=0, keepdims=True)
    part[0:1] = energy
    part[1:2] = moment
    part_copies = [
        pltpu.make_async_remote_copy(
            src_ref=part,
            dst_ref=parts.at[hop - 1],
            send_sem=part_send.at[hop - 1],
            recv_sem=part_recv.at[hop - 1],
            device_id=(tile, comp_at[hop]),
            device_id_type=MESH,
        )
        for hop in (2, 1, 3)
    ]
    for copy in part_copies:
        copy.start()

    def refracted(d):
        values = spec[d * NK : (d + 1) * NK]
        before = ghost[0] if d == 0 else spec[(d - 1) * NK : d * NK]
        beyond = ghost[1] if d == DIRS - 1 else spec[(d + 1) * NK : (d + 2) * NK]
        return values - jnp.abs(turn) * (values - jnp.where(turn > 0, before, beyond))

    def grow(d):
        span = slice(d * NK, (d + 1) * NK)
        gain[span] = gain[span] * shifted(refracted(d))

    for d in range(1, DIRS - 1):
        grow(d)
    ghost_copies[0].wait_recv()
    grow(0)
    ghost_copies[1].wait_recv()
    grow(DIRS - 1)
    for copy in part_copies:
        copy.wait_recv()
    whole = (part[...] + parts[0] + parts[1] + parts[2]) * jnp.float32(1.0 / COMPS)
    energy = whole[0:1]
    mean_freq = whole[1:2] / jnp.maximum(energy, 0.05)
    strength = mean_freq * mean_freq * mean_freq * energy * energy
    damping = 0.005 * (sigma * sigma) * strength
    factor = 1.0 / (1.0 + damping)
    for d in range(DIRS):
        span = slice(d * NK, (d + 1) * NK)
        out_ref[span] = gain[span] * factor

    for copy in ghost_copies + part_copies:
        copy.wait_send()
    pl.when(has_far)(lambda: spot_copy.wait_send())
    for level in range(NSUB):
        for side in (NEAR, FAR):
            for group in range(len(GROUPS)):
                only_if_far(side, lambda: halo_copy(level, side, group).wait_send())


def shards(
    action,
    speed_courant,
    turning,
    freq_shift,
    wind_speed,
    wind_dir,
    sea_mask,
    neighbours,
    halo_rows,
):
    vmem = pltpu.VMEM
    f32 = jnp.float32
    dma = pltpu.SemaphoreType.DMA
    groups = len(GROUPS)

    def row(values):
        return values.reshape(1, values.shape[0])

    return pl.pallas_call(
        kernel,
        out_shape=jax.ShapeDtypeStruct((ROWS, PTS), f32),
        in_specs=[pl.BlockSpec(memory_space=pltpu.HBM)] * 9,
        out_specs=pl.BlockSpec(memory_space=pltpu.VMEM),
        scratch_shapes=[
            vmem((ROWS, PTS), f32),
            vmem((1, NK), f32),
            vmem((1, PTS), f32),
            vmem((1, PTS), f32),
            vmem((1, PTS), f32),
            vmem((1, PTS), f32),
            vmem((1, PTS), jnp.int32),
            vmem((4, PTS), jnp.int32),
            vmem((1, 2 * RIM), jnp.int32),
            vmem((EXT, OWN_N), jnp.bfloat16),
            vmem((EXT, SEND_N), jnp.bfloat16),
            vmem((RIM, 2 * RIM), jnp.bfloat16),
            vmem((ROWS, RIM), f32),
            vmem((ROWS, RIM), f32),
            vmem((ROWS, RIM), f32),
            vmem((NSUB, 2, ROWS, RIM), f32),
            vmem((NSUB, 2, ROWS, RIM), f32),
            vmem((ROWS, PTS), f32),
            vmem((2, ROWS, RIM), f32),
            vmem((ROWS, RIM), f32),
            vmem((ROWS, PTS), f32),
            vmem((2, NK, PTS), f32),
            vmem((2, PTS), f32),
            vmem((3, 2, PTS), f32),
            vmem((1, 2 * RIM), f32),
            vmem((1, 2 * RIM), f32),
            dma((9,)),
            dma((NSUB, 2, groups)),
            dma((NSUB, 2, groups)),
            dma((2,)),
            dma((2,)),
            dma((3,)),
            dma((3,)),
            dma,
            dma,
        ],
        compiler_params=pltpu.CompilerParams(
            collective_id=0, has_side_effects=True, vmem_limit_bytes=60 * 1024 * 1024
        ),
        name="wave_step",
    )(
        action,
        row(speed_courant),
        row(turning),
        row(freq_shift),
        row(wind_speed),
        row(wind_dir),
        row(sea_mask),
        neighbours,
        row(halo_rows),
    )


def solution(mesh):
    placed = (
        P("comp", "tiles"),
        P(),
        P("tiles"),
        P("tiles"),
        P("tiles"),
        P("tiles"),
        P("tiles"),
        P(None, "tiles"),
        P("tiles"),
    )
    return jax.shard_map(
        shards, mesh=mesh, in_specs=placed, out_specs=P("comp", "tiles"), check_vma=False
    )
```

```python
import functools
import math

import jax
import jax.numpy as jnp
import numpy as np
from jax import lax
from jax.experimental import pallas as pl
from jax.experimental.pallas import tpu as pltpu
from jax.sharding import PartitionSpec as P

NSUB = 4
NTH = 24
NK = 32
PTS = 512
RIM = 128
EXT = PTS + 2 * RIM
COMP_AXIS = 4
DIRS = NTH // COMP_AXIS
ROWS = DIRS * NK
COMPS = NTH * NK
OWN_N = 2 * PTS
NEAR, FAR = 0, 1
GROUPS = ((0, 6),)
MESH = pl.DeviceIdType.MESH
STEP = np.float32(2.0 * math.pi / NTH)
LOG_RATIO = np.float32(math.log(1.1))


def pick(index, values):
    chosen = jnp.float32(values[0])
    for place in range(1, len(values)):
        chosen = jnp.where(index == place, jnp.float32(values[place]), chosen)
    return chosen


def halves(values):
    high = values.astype(jnp.bfloat16)
    low = (values - high.astype(jnp.float32)).astype(jnp.bfloat16)
    return jnp.concatenate([high, low], axis=0)


def gathered(split, table):
    both = jnp.dot(split, table, preferred_element_type=jnp.float32)
    rows = both.shape[0] // 2
    return both[:rows] + both[rows:]


def wide(column, lanes):
    return jnp.concatenate([column] * (lanes // RIM), axis=1)


def onehot(first, count, index):
    places = lax.broadcasted_iota(jnp.int32, (count, index.shape[1]), 0) + first
    return jnp.where(places == index, 1.0, 0.0).astype(jnp.bfloat16)


def kernel(
    row_of_tiles,
    action_hbm,
    speed_hbm,
    turning_hbm,
    shift_hbm,
    wind_hbm,
    dir_hbm,
    mask_hbm,
    links_hbm,
    rows_hbm,
    out_ref,
    spec,
    speed,
    turning,
    shift,
    wind,
    wdir,
    mask,
    links,
    rows,
    table,
    send_table,
    back_table,
    across,
    along,
    keep,
    outgoing,
    rim,
    pending,
    pending_send,
    lists,
    mended,
    gain,
    ghost,
    part,
    parts,
    spots,
    back_spots,
    load_sem,
    halo_send,
    halo_recv,
    ghost_send,
    ghost_recv,
    part_send,
    part_recv,
    spot_send,
    spot_recv,
    two_on,
):
    tile = lax.axis_index("tiles")
    comp = lax.axis_index("comp")
    tiles = lax.axis_size("tiles")
    first_core = lax.rem(tile, 2) == 0
    near_tile = jnp.where(first_core, tile + 1, tile - 1)
    far_tile = jnp.where(first_core, tile - 1, tile + 1)
    has_far = jnp.logical_and(far_tile >= 0, far_tile < tiles)
    far_tile = jnp.clip(far_tile, 0, tiles - 1)
    comp_at = [lax.rem(comp + step, COMP_AXIS) for step in range(COMP_AXIS)]

    barrier = pltpu.get_barrier_semaphore()
    for place in (
        (near_tile, comp),
        (tile, comp_at[1]),
        (tile, comp_at[3]),
    ):
        pl.semaphore_signal(barrier, inc=1, device_id=place, device_id_type=MESH)

    @pl.when(has_far)
    def _():
        pl.semaphore_signal(barrier, inc=1, device_id=(far_tile, comp), device_id_type=MESH)

    loads = [
        pltpu.make_async_copy(source, target, load_sem.at[number])
        for number, (source, target) in enumerate(
            (
                (rows_hbm, rows),
                (mask_hbm, mask),
                (action_hbm, spec),
                (links_hbm, links),
                (speed_hbm, speed),
                (turning_hbm, turning),
                (shift_hbm, shift),
                (wind_hbm, wind),
                (dir_hbm, wdir),
            )
        )
    ]
    for load in loads:
        load.start()

    def span_of(group):
        return slice(GROUPS[group][0] * NK, GROUPS[group][1] * NK)

    def tile_at(side):
        if isinstance(side, int):
            return near_tile if side == NEAR else far_tile
        return jnp.where(side == NEAR, near_tile, far_tile)

    def halo_copy(level, side, group):
        first, last = (GROUPS[group][0] * NK, GROUPS[group][1] * NK)
        span = pl.ds(first, last - first)
        return pltpu.make_async_remote_copy(
            src_ref=outgoing.at[level, side, span],
            dst_ref=rim.at[level, side, span],
            send_sem=halo_send.at[level, side, group],
            recv_sem=halo_recv.at[level, side, group],
            device_id=(tile_at(side), comp),
            device_id_type=MESH,
        )

    def only_if_far(side, action):
        if side == NEAR:
            action()
        else:
            pl.when(has_far)(action)

    def send_halo(level, side, group, values):
        outgoing[level, side, span_of(group)] = values
        only_if_far(side, lambda: halo_copy(level, side, group).start())

    def await_halo(level, side, group):
        only_if_far(side, lambda: halo_copy(level, side, group).wait_recv())

    OWN, NEAR_ROWS, FAR_ROWS = (slice(0, PTS), slice(PTS, PTS + RIM), slice(PTS + RIM, EXT))
    RIMS = slice(PTS, EXT)
    SIDES = (FAR, NEAR)
    groups = range(len(GROUPS))

    loads[0].wait()
    low_rows, high_rows = (rows[:, 0:RIM], rows[:, RIM : 2 * RIM])
    near_rows = jnp.where(first_core, high_rows, low_rows)
    far_rows = jnp.where(first_core, low_rows, high_rows)
    picker = onehot(0, PTS, jnp.concatenate([near_rows, far_rows], axis=1))

    loads[1].wait()
    wet = mask[...].astype(jnp.float32)
    loads[3].wait()
    west_side = jnp.logical_or(comp == 0, comp == COMP_AXIS - 1)
    south_side = comp < 2
    near_first = jnp.where(first_core, RIM + PTS, 0)
    far_first = jnp.where(first_core, 0, RIM + PTS)
    for axis, index in enumerate(
        (
            jnp.where(west_side, links[0:1], links[1:2]),
            jnp.where(south_side, links[2:3], links[3:4]),
        )
    ):
        no_left = jnp.logical_and(tile == 0, index < RIM)
        no_right = jnp.logical_and(tile == tiles - 1, index >= RIM + PTS)
        nothing = jnp.logical_or(jnp.logical_or(no_left, no_right), mask[...] == 0)
        index = jnp.where(nothing, EXT, index)
        lanes = pl.ds(axis * PTS, PTS)
        table[0:PTS, lanes] = onehot(RIM, PTS, index)
        table[PTS : PTS + RIM, lanes] = onehot(near_first, RIM, index)
        table[PTS + RIM : EXT, lanes] = onehot(far_first, RIM, index)
    counted = lax.broadcasted_iota(jnp.int32, (RIM, RIM), 0).astype(jnp.float32)
    for axis in range(2):
        picked = jnp.dot(
            table[:, axis * PTS : (axis + 1) * PTS], picker, preferred_element_type=jnp.float32
        )
        for side in (NEAR, FAR):
            lanes = slice(RIM * axis, RIM * (axis + 1))
            chosen = picked[:, side * RIM : (side + 1) * RIM]
            send_table[side, :, lanes] = chosen.astype(jnp.bfloat16)
        for side, places in ((NEAR, NEAR_ROWS), (FAR, FAR_ROWS)):
            block = picked[places, side * RIM : (side + 1) * RIM]
            spots[side, :, axis * RIM : (axis + 1) * RIM] = float(RIM) + jnp.sum(
                block * (counted - float(RIM)), axis=0, keepdims=True
            )

    loads[4].wait()
    diagonal = lax.broadcasted_iota(jnp.int32, (NK, NK), 0) == lax.broadcasted_iota(
        jnp.int32, (NK, NK), 1
    )
    courant = jnp.sum(jnp.where(diagonal, speed[...], 0.0), axis=1, keepdims=True)
    courant = jnp.broadcast_to(courant, (NK, RIM))
    angles = np.arange(NTH).astype(np.float32) * STEP
    cosines = np.abs(np.cos(angles)).reshape(COMP_AXIS, DIRS)
    sines = np.abs(np.sin(angles)).reshape(COMP_AXIS, DIRS)
    for d in range(DIRS):
        span = slice(d * NK, (d + 1) * NK)
        speed_x = courant * pick(comp, cosines[:, d])
        speed_y = courant * pick(comp, sines[:, d])
        across[span] = speed_x
        along[span] = speed_y
        keep[span] = 1.0 - speed_x - speed_y

    def weighed(span, picked):
        lanes = picked.shape[1] // 2
        return (
            wide(across[span], lanes) * picked[:, :lanes]
            + wide(along[span], lanes) * picked[:, lanes:]
        )

    def from_points(span, split, places):
        return weighed(span, gathered(split, table[places, :]))

    def from_sends(span, split, places, side):
        return weighed(span, gathered(split, send_table[side, places]))

    def own_points(span, split, values):
        pending[span] = wide(keep[span], PTS) * values + from_points(span, split, OWN)

    def own_sends(level, span, split, side, values):
        lists[side, span] = values
        pending_send[level % 2, side, span] = keep[span] * values + from_sends(
            span, split, OWN, side
        )

    def mend(span, side):
        return weighed(span, gathered(halves(lists[side, span]), back_table[side]))

    loads[2].wait()
    spec[...] = spec[...] * wet
    splits = []
    for group in groups:
        split = halves(spec[span_of(group)])
        splits.append(split)
        first = gathered(split, picker)
        outgoing[0, NEAR, span_of(group)] = first[:, :RIM]
        outgoing[0, FAR, span_of(group)] = first[:, RIM:]
    for group in groups:
        for side in SIDES:
            own_sends(0, span_of(group), splits[group], side, outgoing[0, side, span_of(group)])

    @pl.when(jnp.logical_not(has_far))
    def _():
        for level in range(NSUB):
            rim[level, FAR] = jnp.zeros((ROWS, RIM), jnp.float32)
        back_spots[FAR] = jnp.full((1, 2 * RIM), float(RIM), jnp.float32)

    spot_copies = [
        pltpu.make_async_remote_copy(
            src_ref=spots.at[side],
            dst_ref=back_spots.at[side],
            send_sem=spot_send.at[side],
            recv_sem=spot_recv.at[side],
            device_id=(near_tile if side == NEAR else far_tile, comp),
            device_id_type=MESH,
        )
        for side in (NEAR, FAR)
    ]

    pl.semaphore_wait(barrier, jnp.where(has_far, 4, 3))
    for side in SIDES:
        only_if_far(side, lambda: spot_copies[side].start())
        for group in groups:
            only_if_far(side, lambda: halo_copy(0, side, group).start())

    pl.semaphore_signal(two_on, inc=1, device_id=(tile, comp_at[3]), device_id_type=MESH)

    ghost_copies = [
        pltpu.make_async_remote_copy(
            src_ref=spec.at[pl.ds(at * NK, NK)],
            dst_ref=ghost.at[slot],
            send_sem=ghost_send.at[slot],
            recv_sem=ghost_recv.at[slot],
            device_id=(tile, target),
            device_id_type=MESH,
        )
        for slot, at, target in ((0, DIRS - 1, comp_at[1]), (1, 0, comp_at[3]))
    ]

    spans = [span_of(group) for group in groups]

    def whole_rim(level, side, group):
        values = rim[level, side, spans[group]]
        if (level, side) in ((1, FAR), (2, FAR), (2, NEAR), (3, FAR)):
            values = values + mended[side, spans[group]]
        return values

    def arrived(level, side, group):
        await_halo(level, side, group)
        return halves(whole_rim(level, side, group))

    def for_far(level, span, near):
        return pending_send[level % 2, FAR, span] + from_sends(span, near, NEAR_ROWS, FAR)

    def whole_list(level, span, side, both):
        return pending_send[level % 2, side, span] + from_sends(span, both, RIMS, side)

    def joined(near, far):
        return jnp.concatenate([near, far], axis=1)

    def next_points(span, both):
        return pending[span] + from_points(span, both, RIMS)

    near_0 = []
    for group in groups:
        near_0.append(arrived(0, NEAR, group))
        send_halo(1, FAR, group, for_far(0, spans[group], near_0[group]))
    for group, span in enumerate(spans):
        own_points(span, splits[group], spec[span])
    for number in (5, 6, 7, 8):
        loads[number].wait()
    sigma = jnp.exp(
        (lax.broadcasted_iota(jnp.int32, (NK, RIM), 0) - NK // 2).astype(jnp.float32) * LOG_RATIO
    )
    sigma = wide(sigma, PTS)
    angle = (lax.broadcasted_iota(jnp.int32, (8, PTS), 0) + comp * DIRS).astype(jnp.float32) * STEP
    aligned = jnp.cos(angle - wdir[...])
    driven = wind[...] * sigma
    for d in range(DIRS):
        grown = 0.4 * jnp.maximum(driven * aligned[d : d + 1] - 0.3, 0.0)
        gain[d * NK : (d + 1) * NK] = wet * (1.0 + grown)
    places = lax.broadcasted_iota(jnp.int32, (RIM, 2 * RIM), 0).astype(jnp.float32)
    for side in SIDES:
        only_if_far(side, lambda: spot_copies[side].wait_recv())
        back_table[side] = jnp.where(places == back_spots[side], 1.0, 0.0).astype(jnp.bfloat16)
    for span in spans:
        mended[FAR, span] = mend(span, FAR)
    split_1 = []
    points_1 = []
    near_list_1 = []
    for group, span in enumerate(spans):
        both = joined(near_0[group], arrived(0, FAR, group))
        near_list_1.append(whole_list(0, span, NEAR, both))
        far_list_1 = whole_list(0, span, FAR, both)
        points_1.append(next_points(span, both))
        send_halo(1, NEAR, group, near_list_1[group])
        split_1.append(halves(points_1[group]))
        own_sends(1, span, split_1[group], FAR, far_list_1)

    can_wait = lax.rem(tile, row_of_tiles) == row_of_tiles - 1

    def near_list_work():
        for group, span in enumerate(spans):
            own_sends(1, span, split_1[group], NEAR, near_list_1[group])

    pl.when(jnp.logical_not(can_wait))(near_list_work)
    first_side = jnp.where(first_core, FAR, NEAR)

    def await_side(side):
        for group in groups:
            pl.when(jnp.logical_or(side == NEAR, has_far))(
                lambda: halo_copy(1, side, group).wait_recv()
            )

    def send_past(side):
        other = 1 - side
        for group, span in enumerate(spans):
            share = jnp.where(side == FAR, mended[FAR, span], 0.0)
            split = halves(rim[1, side, span] + share)
            rows_of_side = pl.ds(pl.multiple_of(PTS + RIM * side, RIM), RIM)
            outgoing[2, other, span] = pending_send[1, other, span] + weighed(
                span, gathered(split, send_table[other, rows_of_side])
            )
            pl.when(jnp.logical_or(other == NEAR, has_far))(
                lambda: halo_copy(2, other, group).start()
            )

    await_side(first_side)
    send_past(first_side)
    await_side(1 - first_side)
    pl.when(jnp.logical_not(can_wait))(lambda: send_past(1 - first_side))
    points_2 = []
    split_2 = []
    near_1 = []
    both_1 = []
    for group, span in enumerate(spans):
        near_1.append(halves(whole_rim(1, NEAR, group)))
        both_1.append(joined(near_1[group], halves(whole_rim(1, FAR, group))))
        values = wide(keep[span], PTS) * points_1[group] + from_points(
            span, joined(split_1[group], both_1[group]), slice(0, EXT)
        )
        whole = whole_list(1, span, FAR, both_1[group])
        points_2.append(values)
        split_2.append(halves(values))
        far_share = mend(span, FAR)
        mended[FAR, span] = far_share
        own_sends(2, span, split_2[group], FAR, whole)
        lists[NEAR, span] = near_list_1[group]
        mended[NEAR, span] = mend(span, NEAR)

    near_2 = []
    for group, span in enumerate(spans):
        near_2.append(arrived(2, NEAR, group))
        send_halo(3, FAR, group, for_far(2, span, near_2[group]))

    @pl.when(can_wait)
    def _():
        near_list_work()
        for group, span in enumerate(spans):
            far = both_1[group][:, RIM:]
            sends = pending_send[1, NEAR, span] + from_sends(span, far, FAR_ROWS, NEAR)
            send_halo(2, NEAR, group, sends)

    for group, span in enumerate(spans):
        near_list_2 = whole_list(1, span, NEAR, both_1[group])
        own_sends(2, span, split_2[group], NEAR, near_list_2)
        own_points(span, split_2[group], points_2[group])
    for group, span in enumerate(spans):
        both = joined(near_2[group], arrived(2, FAR, group))
        sends = whole_list(2, span, NEAR, both)
        values = next_points(span, both)
        send_halo(3, NEAR, group, sends)
        own_points(span, halves(values), values)
        mended[FAR, span] = mend(span, FAR)

    near_3 = [arrived(3, NEAR, group) for group in groups]
    far_3 = [arrived(3, FAR, group) for group in groups]
    for group, (low, high) in enumerate(GROUPS):
        span = spans[group]
        spec[span] = next_points(span, joined(near_3[group], far_3[group]))
        if low == 0:
            ghost_copies[1].start()
        if high == DIRS:
            ghost_copies[0].start()

    turn = turning[...]
    moved = shift[...]
    freq = lax.broadcasted_iota(jnp.int32, (NK, PTS), 0)

    def shifted(values):
        lower = jnp.where(freq == 0, 0.0, pltpu.roll(values, 1, 0))
        upper = jnp.where(freq == NK - 1, 0.0, pltpu.roll(values, NK - 1, 0))
        return values - jnp.abs(moved) * (values - jnp.where(moved > 0, lower, upper))

    total = spec[0:NK]
    for d in range(1, DIRS):
        total = total + spec[d * NK : (d + 1) * NK]
    total = shifted(total) * sigma
    energy = jnp.sum(total, axis=0, keepdims=True)
    moment = jnp.sum(total * sigma, axis=0, keepdims=True)
    part[0:1] = energy
    part[1:2] = moment
    part_copies = [
        pltpu.make_async_remote_copy(
            src_ref=part,
            dst_ref=parts.at[hop - 1],
            send_sem=part_send.at[hop - 1],
            recv_sem=part_recv.at[hop - 1],
            device_id=(tile, comp_at[hop]),
            device_id_type=MESH,
        )
        for hop in (2, 1, 3)
    ]
    pl.semaphore_wait(two_on, 1)
    for copy in part_copies:
        copy.start()

    def refracted(d):
        values = spec[d * NK : (d + 1) * NK]
        before = ghost[0] if d == 0 else spec[(d - 1) * NK : d * NK]
        beyond = ghost[1] if d == DIRS - 1 else spec[(d + 1) * NK : (d + 2) * NK]
        return values - jnp.abs(turn) * (values - jnp.where(turn > 0, before, beyond))

    def grow(d):
        span = slice(d * NK, (d + 1) * NK)
        gain[span] = gain[span] * shifted(refracted(d))

    for d in range(1, DIRS - 1):
        grow(d)
    for copy in ghost_copies + part_copies:
        copy.wait_send()
    for side in SIDES:
        only_if_far(side, lambda: spot_copies[side].wait_send())
    for level in range(NSUB):
        for side in (NEAR, FAR):
            for group in range(len(GROUPS)):
                only_if_far(side, lambda: halo_copy(level, side, group).wait_send())
    ghost_copies[0].wait_recv()
    grow(0)
    ghost_copies[1].wait_recv()
    grow(DIRS - 1)
    for copy in part_copies:
        copy.wait_recv()
    whole = (part[...] + parts[0] + parts[1] + parts[2]) * jnp.float32(1.0 / COMPS)
    energy = whole[0:1]
    mean_freq = whole[1:2] / jnp.maximum(energy, 0.05)
    strength = mean_freq * mean_freq * mean_freq * energy * energy
    damping = 0.005 * (sigma * sigma) * strength
    factor = 1.0 / (1.0 + damping)
    for d in range(DIRS):
        span = slice(d * NK, (d + 1) * NK)
        out_ref[span] = gain[span] * factor


def shards(
    row_of_tiles,
    action,
    speed_courant,
    turning,
    freq_shift,
    wind_speed,
    wind_dir,
    sea_mask,
    neighbours,
    halo_rows,
):
    vmem = pltpu.VMEM
    f32 = jnp.float32
    dma = pltpu.SemaphoreType.DMA
    groups = len(GROUPS)

    def row(values):
        return values.reshape(1, values.shape[0])

    return pl.pallas_call(
        functools.partial(kernel, row_of_tiles),
        out_shape=pltpu.VMEM((ROWS, PTS), f32),
        in_specs=[pl.BlockSpec(memory_space=pltpu.HBM)] * 9,
        out_specs=pl.BlockSpec(memory_space=pltpu.VMEM),
        scratch_shapes=[
            vmem((ROWS, PTS), f32),
            vmem((1, NK), f32),
            vmem((1, PTS), f32),
            vmem((1, PTS), f32),
            vmem((1, PTS), f32),
            vmem((1, PTS), f32),
            vmem((1, PTS), jnp.int32),
            vmem((4, PTS), jnp.int32),
            vmem((1, 2 * RIM), jnp.int32),
            vmem((EXT, OWN_N), jnp.bfloat16),
            vmem((2, EXT, 2 * RIM), jnp.bfloat16),
            vmem((2, RIM, 2 * RIM), jnp.bfloat16),
            vmem((ROWS, RIM), f32),
            vmem((ROWS, RIM), f32),
            vmem((ROWS, RIM), f32),
            vmem((NSUB, 2, ROWS, RIM), f32),
            vmem((NSUB, 2, ROWS, RIM), f32),
            vmem((ROWS, PTS), f32),
            vmem((2, 2, ROWS, RIM), f32),
            vmem((2, ROWS, RIM), f32),
            vmem((2, ROWS, RIM), f32),
            vmem((ROWS, PTS), f32),
            vmem((2, NK, PTS), f32),
            vmem((2, PTS), f32),
            vmem((3, 2, PTS), f32),
            vmem((2, 1, 2 * RIM), f32),
            vmem((2, 1, 2 * RIM), f32),
            dma((9,)),
            dma((NSUB, 2, groups)),
            dma((NSUB, 2, groups)),
            dma((2,)),
            dma((2,)),
            dma((3,)),
            dma((3,)),
            dma((2,)),
            dma((2,)),
            pltpu.SemaphoreType.REGULAR,
        ],
        compiler_params=pltpu.CompilerParams(
            collective_id=0, has_side_effects=True, vmem_limit_bytes=48 * 1024 * 1024
        ),
        name="wave_step",
    )(
        *(
            pltpu.with_memory_space_constraint(values, pltpu.HBM)
            for values in (
                action,
                row(speed_courant),
                row(turning),
                row(freq_shift),
                row(wind_speed),
                row(wind_dir),
                row(sea_mask),
                neighbours,
                row(halo_rows),
            )
        )
    )


def solution(mesh):
    placed = (
        P("comp", "tiles"),
        P(),
        P("tiles"),
        P("tiles"),
        P("tiles"),
        P("tiles"),
        P("tiles"),
        P(None, "tiles"),
        P("tiles"),
    )
    return jax.shard_map(
        functools.partial(shards, mesh.shape["tiles"] // COMP_AXIS), mesh=mesh, in_specs=placed, out_specs=P("comp", "tiles"), check_vma=False
    )
```

```python
import functools
import math

import jax
import jax.numpy as jnp
import numpy as np
from jax import lax
from jax.experimental import pallas as pl
from jax.experimental.pallas import tpu as pltpu
from jax.sharding import PartitionSpec as P

NSUB = 4
NTH = 24
NK = 32
PTS = 512
RIM = 128
EXT = PTS + 2 * RIM
COMP_AXIS = 4
DIRS = NTH // COMP_AXIS
ROWS = DIRS * NK
COMPS = NTH * NK
OWN_N = 2 * PTS
NEAR, FAR = 0, 1
SPOT_ROWS = 8
MESH = pl.DeviceIdType.MESH
STEP = np.float32(2.0 * math.pi / NTH)
LOG_RATIO = np.float32(math.log(1.1))


def pick(index, values):
    chosen = jnp.float32(values[0])
    for place in range(1, len(values)):
        chosen = jnp.where(index == place, jnp.float32(values[place]), chosen)
    return chosen


def halves(values):
    high = values.astype(jnp.bfloat16)
    low = (values - high.astype(jnp.float32)).astype(jnp.bfloat16)
    return jnp.concatenate([high, low], axis=0)


def gathered(split, table):
    both = jnp.dot(split, table, preferred_element_type=jnp.float32)
    rows = both.shape[0] // 2
    return both[:rows] + both[rows:]


def wide(column, lanes):
    return jnp.concatenate([column] * (lanes // RIM), axis=1)


def onehot(first, count, index):
    places = lax.broadcasted_iota(jnp.int32, (count, index.shape[1]), 0) + first
    return jnp.where(places == index, 1.0, 0.0).astype(jnp.bfloat16)


def kernel(
    row_of_tiles,
    action_hbm,
    speed_hbm,
    turning_hbm,
    shift_hbm,
    wind_hbm,
    dir_hbm,
    mask_hbm,
    links_hbm,
    rows_hbm,
    out_ref,
    spec,
    speed,
    misc,
    mask,
    links,
    rows,
    table,
    send_table,
    back_table,
    across,
    along,
    keep,
    first_out,
    first_rim,
    outgoing,
    rim,
    pending,
    pending_send,
    lists,
    mended,
    gain,
    ghost,
    part,
    parts,
    local_sem,
    halo_recv,
    ghost_recv,
    part_recv,
    two_on,
):
    tile = lax.axis_index("tiles")
    comp = lax.axis_index("comp")
    tiles = lax.axis_size("tiles")
    first_core = lax.rem(tile, 2) == 0
    near_tile = jnp.where(first_core, tile + 1, tile - 1)
    far_tile = jnp.where(first_core, tile - 1, tile + 1)
    has_far = jnp.logical_and(far_tile >= 0, far_tile < tiles)
    far_tile = jnp.clip(far_tile, 0, tiles - 1)
    comp_at = [lax.rem(comp + step, COMP_AXIS) for step in range(COMP_AXIS)]

    barrier = pltpu.get_barrier_semaphore()
    for place in (
        (near_tile, comp),
        (tile, comp_at[1]),
        (tile, comp_at[3]),
    ):
        pl.semaphore_signal(barrier, inc=1, device_id=place, device_id_type=MESH)

    @pl.when(has_far)
    def _():
        pl.semaphore_signal(barrier, inc=1, device_id=(far_tile, comp), device_id_type=MESH)

    loads = [
        pltpu.make_async_copy(source, target, local_sem.at[number])
        for number, source, target in (
            (0, rows_hbm, rows),
            (1, mask_hbm, mask),
            (2, action_hbm, spec),
            (3, links_hbm, links),
            (4, speed_hbm, speed),
            (5, turning_hbm, misc.at[pl.ds(0, 1)]),
            (5, shift_hbm, misc.at[pl.ds(1, 1)]),
            (5, wind_hbm, misc.at[pl.ds(2, 1)]),
            (5, dir_hbm, misc.at[pl.ds(3, 1)]),
        )
    ]
    for load in loads:
        load.start()

    def await_bytes(ref, semaphore):
        pltpu.make_async_copy(ref, ref, semaphore).wait()

    near_sent, far_sent, ghost_sent, first_near_sent, first_far_sent, part_sent = (
        local_sem.at[number] for number in range(6)
    )

    def tile_at(side):
        if isinstance(side, int):
            return near_tile if side == NEAR else far_tile
        return jnp.where(side == NEAR, near_tile, far_tile)

    def halo_copy(level, side):
        if level == 0:
            source, target = (first_out.at[side], first_rim.at[side])
            sent = first_near_sent if side == NEAR else first_far_sent
        else:
            source, target = (outgoing.at[level - 1, side], rim.at[level - 1, side])
            sent = local_sem.at[side]
        return pltpu.make_async_remote_copy(
            src_ref=source,
            dst_ref=target,
            send_sem=sent,
            recv_sem=halo_recv.at[level, side],
            device_id=(tile_at(side), comp),
            device_id_type=MESH,
        )

    def only_if_far(side, action):
        if side == NEAR:
            action()
        else:
            pl.when(has_far)(action)

    def send_halo(level, side, values):
        outgoing[level - 1, side] = values
        only_if_far(side, lambda: halo_copy(level, side).start())

    def await_halo(level, side):
        only_if_far(side, lambda: halo_copy(level, side).wait_recv())

    OWN, NEAR_ROWS, FAR_ROWS = (slice(0, PTS), slice(PTS, PTS + RIM), slice(PTS + RIM, EXT))
    RIMS = slice(PTS, EXT)
    SIDES = (FAR, NEAR)

    loads[0].wait()
    low_rows, high_rows = (rows[:, 0:RIM], rows[:, RIM : 2 * RIM])
    near_rows = jnp.where(first_core, high_rows, low_rows)
    far_rows = jnp.where(first_core, low_rows, high_rows)
    picker = onehot(0, PTS, jnp.concatenate([near_rows, far_rows], axis=1))

    loads[1].wait()
    wet = mask[...].astype(jnp.float32)
    loads[3].wait()
    west_side = jnp.logical_or(comp == 0, comp == COMP_AXIS - 1)
    south_side = comp < 2
    near_first = jnp.where(first_core, RIM + PTS, 0)
    far_first = jnp.where(first_core, 0, RIM + PTS)
    for axis, index in enumerate(
        (
            jnp.where(west_side, links[0:1], links[1:2]),
            jnp.where(south_side, links[2:3], links[3:4]),
        )
    ):
        no_left = jnp.logical_and(tile == 0, index < RIM)
        no_right = jnp.logical_and(tile == tiles - 1, index >= RIM + PTS)
        nothing = jnp.logical_or(jnp.logical_or(no_left, no_right), mask[...] == 0)
        index = jnp.where(nothing, EXT, index)
        lanes = pl.ds(axis * PTS, PTS)
        table[0:PTS, lanes] = onehot(RIM, PTS, index)
        table[PTS : PTS + RIM, lanes] = onehot(near_first, RIM, index)
        table[PTS + RIM : EXT, lanes] = onehot(far_first, RIM, index)
    counted = lax.broadcasted_iota(jnp.int32, (RIM, RIM), 0).astype(jnp.float32)
    for axis in range(2):
        picked = jnp.dot(
            table[:, axis * PTS : (axis + 1) * PTS], picker, preferred_element_type=jnp.float32
        )
        for side in (NEAR, FAR):
            lanes = slice(RIM * axis, RIM * (axis + 1))
            chosen = picked[:, side * RIM : (side + 1) * RIM]
            send_table[side, :, lanes] = chosen.astype(jnp.bfloat16)
        for side, places in ((NEAR, NEAR_ROWS), (FAR, FAR_ROWS)):
            block = picked[places, side * RIM : (side + 1) * RIM]
            first_out[side, ROWS + axis : ROWS + axis + 1] = float(RIM) + jnp.sum(
                block * (counted - float(RIM)), axis=0, keepdims=True
            )

    loads[4].wait()
    diagonal = lax.broadcasted_iota(jnp.int32, (NK, NK), 0) == lax.broadcasted_iota(
        jnp.int32, (NK, NK), 1
    )
    courant = jnp.sum(jnp.where(diagonal, speed[...], 0.0), axis=1, keepdims=True)
    courant = jnp.broadcast_to(courant, (NK, RIM))
    angles = np.arange(NTH).astype(np.float32) * STEP
    cosines = np.abs(np.cos(angles)).reshape(COMP_AXIS, DIRS)
    sines = np.abs(np.sin(angles)).reshape(COMP_AXIS, DIRS)
    for d in range(DIRS):
        span = slice(d * NK, (d + 1) * NK)
        speed_x = courant * pick(comp, cosines[:, d])
        speed_y = courant * pick(comp, sines[:, d])
        across[span] = speed_x
        along[span] = speed_y
        keep[span] = 1.0 - speed_x - speed_y

    def weighed(picked):
        lanes = picked.shape[1] // 2
        return (
            wide(across[...], lanes) * picked[:, :lanes]
            + wide(along[...], lanes) * picked[:, lanes:]
        )

    def from_points(split, places):
        return weighed(gathered(split, table[places, :]))

    def from_sends(split, places, side):
        return weighed(gathered(split, send_table[side, places]))

    def own_points(split, values):
        pending[...] = wide(keep[...], PTS) * values + from_points(split, OWN)

    def own_sends(level, split, side, values):
        lists[side] = values
        pending_send[level % 2, side] = keep[...] * values + from_sends(split, OWN, side)

    def mend(side):
        return weighed(gathered(halves(lists[side]), back_table[side]))

    loads[2].wait()
    spec[...] = spec[...] * wet
    split_0 = halves(spec[...])
    first = gathered(split_0, picker)
    for side in SIDES:
        first_out[side, 0:ROWS] = first[:, side * RIM : (side + 1) * RIM]
        first_out[side, ROWS + 2 :] = jnp.zeros((SPOT_ROWS - 2, RIM), jnp.float32)
        own_sends(0, split_0, side, first[:, side * RIM : (side + 1) * RIM])

    @pl.when(jnp.logical_not(has_far))
    def _():
        for level in range(1, NSUB):
            rim[level - 1, FAR] = jnp.zeros((ROWS, RIM), jnp.float32)
        first_rim[FAR, 0:ROWS] = jnp.zeros((ROWS, RIM), jnp.float32)
        first_rim[FAR, ROWS:] = jnp.full((SPOT_ROWS, RIM), float(RIM), jnp.float32)

    pl.semaphore_wait(barrier, jnp.where(has_far, 4, 3))
    for side in SIDES:
        only_if_far(side, lambda: halo_copy(0, side).start())

    pl.semaphore_signal(two_on, inc=1, device_id=(tile, comp_at[3]), device_id_type=MESH)

    ghost_copies = [
        pltpu.make_async_remote_copy(
            src_ref=spec.at[pl.ds(at * NK, NK)],
            dst_ref=ghost.at[slot],
            send_sem=ghost_sent,
            recv_sem=ghost_recv,
            device_id=(tile, target),
            device_id_type=MESH,
        )
        for slot, at, target in ((0, DIRS - 1, comp_at[1]), (1, 0, comp_at[3]))
    ]

    def whole_rim(level, side):
        if level == 0:
            return first_rim[side, 0:ROWS]
        values = rim[level - 1, side]
        if (level, side) in ((1, FAR), (2, FAR), (2, NEAR), (3, FAR)):
            values = values + mended[side]
        return values

    def arrived(level, side):
        await_halo(level, side)
        return halves(whole_rim(level, side))

    def for_far(level, near):
        return pending_send[level % 2, FAR] + from_sends(near, NEAR_ROWS, FAR)

    def whole_list(level, side, both):
        return pending_send[level % 2, side] + from_sends(both, RIMS, side)

    def joined(near, far):
        return jnp.concatenate([near, far], axis=1)

    def next_points(both):
        return pending[...] + from_points(both, RIMS)

    near_0 = arrived(0, NEAR)
    send_halo(1, FAR, for_far(0, near_0))
    own_points(split_0, spec[...])
    await_bytes(misc, local_sem.at[5])
    sigma = jnp.exp(
        (lax.broadcasted_iota(jnp.int32, (NK, RIM), 0) - NK // 2).astype(jnp.float32) * LOG_RATIO
    )
    sigma = wide(sigma, PTS)
    angle = (lax.broadcasted_iota(jnp.int32, (8, PTS), 0) + comp * DIRS).astype(jnp.float32) * STEP
    aligned = jnp.cos(angle - misc[3:4])
    driven = misc[2:3] * sigma
    for d in range(DIRS):
        grown = 0.4 * jnp.maximum(driven * aligned[d : d + 1] - 0.3, 0.0)
        gain[d * NK : (d + 1) * NK] = wet * (1.0 + grown)
    far_0 = arrived(0, FAR)
    both_0 = joined(near_0, far_0)
    near_list_1 = whole_list(0, NEAR, both_0)
    far_list_1 = whole_list(0, FAR, both_0)
    points_1 = next_points(both_0)
    send_halo(1, NEAR, near_list_1)
    split_1 = halves(points_1)
    own_first = lists[FAR]
    own_sends(1, split_1, FAR, far_list_1)
    places = lax.broadcasted_iota(jnp.int32, (RIM, RIM), 0).astype(jnp.float32)
    for side in SIDES:
        for axis in range(2):
            spots = first_rim[side, ROWS + axis : ROWS + axis + 1]
            back_table[side, :, axis * RIM : (axis + 1) * RIM] = jnp.where(
                places == spots, 1.0, 0.0
            ).astype(jnp.bfloat16)
    mended[FAR] = weighed(gathered(halves(own_first), back_table[FAR]))

    can_wait = lax.rem(tile, row_of_tiles) == row_of_tiles - 1

    def near_list_work():
        own_sends(1, split_1, NEAR, near_list_1)

    pl.when(jnp.logical_not(can_wait))(near_list_work)
    first_side = jnp.where(first_core, FAR, NEAR)

    def await_side(side):
        pl.when(jnp.logical_or(side == NEAR, has_far))(lambda: halo_copy(1, side).wait_recv())

    def send_past(side):
        other = 1 - side
        share = jnp.where(side == FAR, mended[FAR], 0.0)
        split = halves(rim[0, side] + share)
        rows_of_side = pl.ds(pl.multiple_of(PTS + RIM * side, RIM), RIM)
        outgoing[1, other] = pending_send[1, other] + weighed(
            gathered(split, send_table[other, rows_of_side])
        )
        pl.when(jnp.logical_or(other == NEAR, has_far))(lambda: halo_copy(2, other).start())

    await_side(first_side)
    send_past(first_side)
    await_side(1 - first_side)
    pl.when(jnp.logical_not(can_wait))(lambda: send_past(1 - first_side))
    near_1 = halves(whole_rim(1, NEAR))
    far_1 = halves(whole_rim(1, FAR))
    both_1 = joined(near_1, far_1)
    points_2 = wide(keep[...], PTS) * points_1 + from_points(joined(split_1, both_1), slice(0, EXT))
    far_list_2 = whole_list(1, FAR, both_1)
    split_2 = halves(points_2)
    far_share = mend(FAR)
    mended[FAR] = far_share
    own_sends(2, split_2, FAR, far_list_2)
    lists[NEAR] = near_list_1
    mended[NEAR] = mend(NEAR)

    near_2 = arrived(2, NEAR)
    send_halo(3, FAR, for_far(2, near_2))

    @pl.when(can_wait)
    def _():
        near_list_work()
        send_halo(2, NEAR, pending_send[1, NEAR] + from_sends(far_1, FAR_ROWS, NEAR))

    own_sends(2, split_2, NEAR, whole_list(1, NEAR, both_1))
    own_points(split_2, points_2)
    both_2 = joined(near_2, arrived(2, FAR))
    near_list_3 = whole_list(2, NEAR, both_2)
    points_3 = next_points(both_2)
    send_halo(3, NEAR, near_list_3)
    own_points(halves(points_3), points_3)
    mended[FAR] = mend(FAR)

    near_3 = arrived(3, NEAR)
    spec[...] = next_points(joined(near_3, arrived(3, FAR)))
    for copy in ghost_copies:
        copy.start()

    turn = misc[0:1]
    moved = misc[1:2]
    freq = lax.broadcasted_iota(jnp.int32, (NK, PTS), 0)

    def shifted(values):
        lower = jnp.where(freq == 0, 0.0, pltpu.roll(values, 1, 0))
        upper = jnp.where(freq == NK - 1, 0.0, pltpu.roll(values, NK - 1, 0))
        return values - jnp.abs(moved) * (values - jnp.where(moved > 0, lower, upper))

    total = spec[0:NK]
    for d in range(1, DIRS):
        total = total + spec[d * NK : (d + 1) * NK]
    total = shifted(total) * sigma
    energy = jnp.sum(total, axis=0, keepdims=True)
    moment = jnp.sum(total * sigma, axis=0, keepdims=True)
    part[0:1] = energy
    part[1:2] = moment
    part_copies = [
        pltpu.make_async_remote_copy(
            src_ref=part,
            dst_ref=parts.at[hop - 1],
            send_sem=part_sent,
            recv_sem=part_recv,
            device_id=(tile, comp_at[hop]),
            device_id_type=MESH,
        )
        for hop in (2, 1, 3)
    ]
    pl.semaphore_wait(two_on, 1)
    for copy in part_copies:
        copy.start()

    def refracted(d):
        values = spec[d * NK : (d + 1) * NK]
        before = ghost[0] if d == 0 else spec[(d - 1) * NK : d * NK]
        beyond = ghost[1] if d == DIRS - 1 else spec[(d + 1) * NK : (d + 2) * NK]
        return values - jnp.abs(turn) * (values - jnp.where(turn > 0, before, beyond))

    def grow(d):
        span = slice(d * NK, (d + 1) * NK)
        gain[span] = gain[span] * shifted(refracted(d))

    for d in range(1, DIRS - 1):
        grow(d)
    await_bytes(ghost, ghost_sent)
    await_bytes(parts, part_sent)
    halo_copy(0, NEAR).wait_send()
    await_bytes(outgoing.at[:, NEAR], near_sent)

    @pl.when(has_far)
    def _():
        halo_copy(0, FAR).wait_send()
        await_bytes(outgoing.at[:, FAR], far_sent)

    await_bytes(ghost, ghost_recv)
    grow(0)
    grow(DIRS - 1)
    await_bytes(parts, part_recv)
    whole = (part[...] + parts[0] + parts[1] + parts[2]) * jnp.float32(1.0 / COMPS)
    energy = whole[0:1]
    mean_freq = whole[1:2] / jnp.maximum(energy, 0.05)
    strength = mean_freq * mean_freq * mean_freq * energy * energy
    damping = 0.005 * (sigma * sigma) * strength
    factor = 1.0 / (1.0 + damping)
    for d in range(DIRS):
        span = slice(d * NK, (d + 1) * NK)
        out_ref[span] = gain[span] * factor


def shards(
    row_of_tiles,
    action,
    speed_courant,
    turning,
    freq_shift,
    wind_speed,
    wind_dir,
    sea_mask,
    neighbours,
    halo_rows,
):
    vmem = pltpu.VMEM
    f32 = jnp.float32
    dma = pltpu.SemaphoreType.DMA

    def row(values):
        return values.reshape(1, values.shape[0])

    return pl.pallas_call(
        functools.partial(kernel, row_of_tiles),
        out_shape=pltpu.VMEM((ROWS, PTS), f32),
        in_specs=[pl.BlockSpec(memory_space=pltpu.HBM)] * 9,
        out_specs=pl.BlockSpec(memory_space=pltpu.VMEM),
        scratch_shapes=[
            vmem((ROWS, PTS), f32),
            vmem((1, NK), f32),
            vmem((4, PTS), f32),
            vmem((1, PTS), jnp.int32),
            vmem((4, PTS), jnp.int32),
            vmem((1, 2 * RIM), jnp.int32),
            vmem((EXT, OWN_N), jnp.bfloat16),
            vmem((2, EXT, 2 * RIM), jnp.bfloat16),
            vmem((2, RIM, 2 * RIM), jnp.bfloat16),
            vmem((ROWS, RIM), f32),
            vmem((ROWS, RIM), f32),
            vmem((ROWS, RIM), f32),
            vmem((2, ROWS + SPOT_ROWS, RIM), f32),
            vmem((2, ROWS + SPOT_ROWS, RIM), f32),
            vmem((NSUB - 1, 2, ROWS, RIM), f32),
            vmem((NSUB - 1, 2, ROWS, RIM), f32),
            vmem((ROWS, PTS), f32),
            vmem((2, 2, ROWS, RIM), f32),
            vmem((2, ROWS, RIM), f32),
            vmem((2, ROWS, RIM), f32),
            vmem((ROWS, PTS), f32),
            vmem((2, NK, PTS), f32),
            vmem((2, PTS), f32),
            vmem((3, 2, PTS), f32),
            dma((6,)),
            dma((NSUB, 2)),
            dma,
            dma,
            pltpu.SemaphoreType.REGULAR,
        ],
        compiler_params=pltpu.CompilerParams(
            collective_id=0, has_side_effects=True, vmem_limit_bytes=48 * 1024 * 1024
        ),
        name="wave_step",
    )(
        *(
            pltpu.with_memory_space_constraint(values, pltpu.HBM)
            for values in (
                action,
                row(speed_courant),
                row(turning),
                row(freq_shift),
                row(wind_speed),
                row(wind_dir),
                row(sea_mask),
                neighbours,
                row(halo_rows),
            )
        )
    )


def solution(mesh):
    placed = (
        P("comp", "tiles"),
        P(),
        P("tiles"),
        P("tiles"),
        P("tiles"),
        P("tiles"),
        P("tiles"),
        P(None, "tiles"),
        P("tiles"),
    )
    return jax.shard_map(
        functools.partial(shards, mesh.shape["tiles"] // COMP_AXIS),
        mesh=mesh,
        in_specs=placed,
        out_specs=P("comp", "tiles"),
        check_vma=False,
    )
```

```python
import functools
import math

import jax
import jax.numpy as jnp
import numpy as np
from jax import lax
from jax.experimental import pallas as pl
from jax.experimental.pallas import tpu as pltpu
from jax.sharding import PartitionSpec as P

NSUB = 4
NTH = 24
NK = 32
PTS = 512
RIM = 128
EXT = PTS + 2 * RIM
COMP_AXIS = 4
DIRS = NTH // COMP_AXIS
ROWS = DIRS * NK
COMPS = NTH * NK
OWN_N = 2 * PTS
NEAR, FAR, LAST_FAR = 0, 1, 2
SPOT_ROWS = 8
SUM_ROWS = 16
ENDS = ((0, NK), (ROWS - NK, ROWS))
INNER = ((NK, ROWS - NK),)
MESH = pl.DeviceIdType.MESH
STEP = np.float32(2.0 * math.pi / NTH)
LOG_RATIO = np.float32(math.log(1.1))


def pick(index, values):
    chosen = jnp.float32(values[0])
    for place in range(1, len(values)):
        chosen = jnp.where(index == place, jnp.float32(values[place]), chosen)
    return chosen


def halves(values):
    high = values.astype(jnp.bfloat16)
    low = (values - high.astype(jnp.float32)).astype(jnp.bfloat16)
    return jnp.concatenate([high, low], axis=0)


def gathered(split, table):
    both = jnp.dot(split, table, preferred_element_type=jnp.float32)
    rows = both.shape[0] // 2
    return both[:rows] + both[rows:]


def gathered_both(first, second, table):
    split = jnp.concatenate([halves(first), halves(second)], axis=0)
    both = jnp.dot(split, table, preferred_element_type=jnp.float32)
    rows, more = (first.shape[0], second.shape[0])
    last = both[2 * rows :]
    return both[:rows] + both[rows : 2 * rows], last[:more] + last[more:]


def wide(column, lanes):
    return jnp.concatenate([column] * (lanes // RIM), axis=1)


def onehot(first, count, index):
    places = lax.broadcasted_iota(jnp.int32, (count, index.shape[1]), 0) + first
    return jnp.where(places == index, 1.0, 0.0).astype(jnp.bfloat16)


def kernel(
    row_of_tiles,
    action_hbm,
    speed_hbm,
    turning_hbm,
    shift_hbm,
    wind_hbm,
    dir_hbm,
    mask_hbm,
    links_hbm,
    rows_hbm,
    out_ref,
    spec,
    speed,
    misc,
    mask,
    links,
    rows,
    table,
    send_table,
    back_table,
    across,
    along,
    keep,
    first_out,
    first_rim,
    outgoing,
    rim,
    pending,
    pending_send,
    mended,
    gain,
    ghost,
    part,
    parts,
    sums_out,
    sums_in,
    local_sem,
    halo_recv,
    ghost_recv,
    part_recv,
    last_sent,
    last_recv,
    two_on,
):
    tile = lax.axis_index("tiles")
    comp = lax.axis_index("comp")
    tiles = lax.axis_size("tiles")
    first_core = lax.rem(tile, 2) == 0
    near_tile = jnp.where(first_core, tile + 1, tile - 1)
    far_tile = jnp.where(first_core, tile - 1, tile + 1)
    has_far = jnp.logical_and(far_tile >= 0, far_tile < tiles)
    far_tile = jnp.clip(far_tile, 0, tiles - 1)
    comp_at = [lax.rem(comp + step, COMP_AXIS) for step in range(COMP_AXIS)]

    barrier = pltpu.get_barrier_semaphore()

    @pl.when(has_far)
    def _():
        pl.semaphore_signal(barrier, inc=1, device_id=(far_tile, comp), device_id_type=MESH)

    for place in (
        (near_tile, comp),
        (tile, comp_at[1]),
        (tile, comp_at[3]),
    ):
        pl.semaphore_signal(barrier, inc=1, device_id=place, device_id_type=MESH)

    loads = [
        pltpu.make_async_copy(source, target, local_sem.at[number])
        for number, source, target in (
            (0, rows_hbm, rows),
            (1, mask_hbm, mask),
            (2, action_hbm, spec),
            (3, links_hbm, links),
            (4, speed_hbm, speed),
            (5, turning_hbm, misc.at[pl.ds(0, 1)]),
            (5, shift_hbm, misc.at[pl.ds(1, 1)]),
            (5, wind_hbm, misc.at[pl.ds(2, 1)]),
            (5, dir_hbm, misc.at[pl.ds(3, 1)]),
        )
    ]
    for load in loads:
        load.start()

    def await_bytes(ref, semaphore):
        pltpu.make_async_copy(ref, ref, semaphore).wait()

    near_sent, far_sent, ghost_sent, first_near_sent, first_far_sent, part_sent = (
        local_sem.at[number] for number in range(6)
    )

    def tile_at(side):
        if isinstance(side, int):
            return near_tile if side == NEAR else far_tile
        return jnp.where(side == NEAR, near_tile, far_tile)

    def halo_copy(level, side):
        if level == 0:
            source, target = (first_out.at[side], first_rim.at[side])
            sent = first_near_sent if side == NEAR else first_far_sent
        else:
            source, target = (outgoing.at[level - 1, side], rim.at[level - 1, side])
            sent = local_sem.at[side]
        return pltpu.make_async_remote_copy(
            src_ref=source,
            dst_ref=target,
            send_sem=sent,
            recv_sem=halo_recv.at[level, side],
            device_id=(tile_at(side), comp),
            device_id_type=MESH,
        )

    def only_if_far(side, action):
        if side == NEAR:
            action()
        else:
            pl.when(has_far)(action)

    def send_halo(level, side, values):
        outgoing[level - 1, side] = values
        only_if_far(side, lambda: halo_copy(level, side).start())

    def await_halo(level, side):
        only_if_far(side, lambda: halo_copy(level, side).wait_recv())

    OWN, NEAR_ROWS, FAR_ROWS = (slice(0, PTS), slice(PTS, PTS + RIM), slice(PTS + RIM, EXT))
    RIMS = slice(PTS, EXT)
    SIDES = (FAR, NEAR)

    loads[0].wait()
    low_rows, high_rows = (rows[:, 0:RIM], rows[:, RIM : 2 * RIM])
    near_rows = jnp.where(first_core, high_rows, low_rows)
    far_rows = jnp.where(first_core, low_rows, high_rows)
    picker = onehot(0, PTS, jnp.concatenate([near_rows, far_rows], axis=1))

    loads[1].wait()
    wet = mask[...].astype(jnp.float32)
    loads[3].wait()
    west_side = jnp.logical_or(comp == 0, comp == COMP_AXIS - 1)
    south_side = comp < 2
    near_first = jnp.where(first_core, RIM + PTS, 0)
    far_first = jnp.where(first_core, 0, RIM + PTS)
    for axis, index in enumerate(
        (
            jnp.where(west_side, links[0:1], links[1:2]),
            jnp.where(south_side, links[2:3], links[3:4]),
        )
    ):
        no_left = jnp.logical_and(tile == 0, index < RIM)
        no_right = jnp.logical_and(tile == tiles - 1, index >= RIM + PTS)
        nothing = jnp.logical_or(jnp.logical_or(no_left, no_right), mask[...] == 0)
        index = jnp.where(nothing, EXT, index)
        lanes = pl.ds(axis * PTS, PTS)
        table[0:PTS, lanes] = onehot(RIM, PTS, index)
        table[PTS : PTS + RIM, lanes] = onehot(near_first, RIM, index)
        table[PTS + RIM : EXT, lanes] = onehot(far_first, RIM, index)
    counted = lax.broadcasted_iota(jnp.int32, (RIM, RIM), 0).astype(jnp.float32)
    for axis in range(2):
        picked = jnp.dot(
            table[:, axis * PTS : (axis + 1) * PTS], picker, preferred_element_type=jnp.float32
        )
        for side in (NEAR, FAR):
            lanes = slice(RIM * axis, RIM * (axis + 1))
            chosen = picked[:, side * RIM : (side + 1) * RIM]
            send_table[side, :, lanes] = chosen.astype(jnp.bfloat16)
        for side, places in ((NEAR, NEAR_ROWS), (FAR, FAR_ROWS)):
            block = picked[places, side * RIM : (side + 1) * RIM]
            first_out[side, ROWS + axis : ROWS + axis + 1] = float(RIM) + jnp.sum(
                block * (counted - float(RIM)), axis=0, keepdims=True
            )

    loads[4].wait()
    diagonal = lax.broadcasted_iota(jnp.int32, (NK, NK), 0) == lax.broadcasted_iota(
        jnp.int32, (NK, NK), 1
    )
    courant = jnp.sum(jnp.where(diagonal, speed[...], 0.0), axis=1, keepdims=True)
    courant = jnp.broadcast_to(courant, (NK, RIM))
    angles = np.arange(NTH).astype(np.float32) * STEP
    cosines = np.abs(np.cos(angles)).reshape(COMP_AXIS, DIRS)
    sines = np.abs(np.sin(angles)).reshape(COMP_AXIS, DIRS)
    for d in range(DIRS):
        span = slice(d * NK, (d + 1) * NK)
        speed_x = courant * pick(comp, cosines[:, d])
        speed_y = courant * pick(comp, sines[:, d])
        across[span] = speed_x
        along[span] = speed_y
        keep[span] = 1.0 - speed_x - speed_y

    number = lax.broadcasted_iota(jnp.int32, (NK, RIM), 0)
    sigma_rim = jnp.exp((number - NK // 2).astype(jnp.float32) * LOG_RATIO)
    sigma_up = jnp.exp((number + 1 - NK // 2).astype(jnp.float32) * LOG_RATIO)
    sigma_down = jnp.exp((number - 1 - NK // 2).astype(jnp.float32) * LOG_RATIO)
    sigma_up = jnp.where(number == NK - 1, 0.0, sigma_up)
    sigma_down = jnp.where(number == 0, 0.0, sigma_down)
    weights = (
        sigma_rim,
        sigma_up,
        sigma_down,
        sigma_rim * sigma_rim,
        sigma_up * sigma_up,
        sigma_down * sigma_down,
    )

    def sums(values, shares):
        lanes = values.shape[1]
        total = wide(shares[0:NK], lanes) * values[0:NK]
        for d in range(1, DIRS):
            span = slice(d * NK, (d + 1) * NK)
            total = total + wide(shares[span], lanes) * values[span]
        return [
            jnp.sum(wide(weight, lanes) * total, axis=0, keepdims=True) for weight in weights
        ]

    def upwind_sums(values):
        gap = [jnp.zeros((SUM_ROWS // 2 - len(weights), values.shape[1]), jnp.float32)]
        return jnp.concatenate(sums(values, across) + gap + sums(values, along) + gap, axis=0)

    def weighed(picked):
        lanes = picked.shape[1] // 2
        return (
            wide(across[...], lanes) * picked[:, :lanes]
            + wide(along[...], lanes) * picked[:, lanes:]
        )

    def from_points(split, places):
        return weighed(gathered(split, table[places, :]))

    def from_sends(split, places, side):
        return weighed(gathered(split, send_table[side, places]))

    def own_points(split, values):
        pending[...] = wide(keep[...], PTS) * values + from_points(split, OWN)

    def own_sends(level, split, side, values):
        pending_send[level % 2, side] = keep[...] * values + from_sends(split, OWN, side)

    def mend(side, values):
        return weighed(gathered(halves(values), back_table[side]))

    loads[2].wait()
    spec[...] = spec[...] * wet
    split_0 = halves(spec[...])
    first = gathered(split_0, picker)
    for side in SIDES:
        first_out[side, 0:ROWS] = first[:, side * RIM : (side + 1) * RIM]
        first_out[side, ROWS + 2 :] = jnp.zeros((SPOT_ROWS - 2, RIM), jnp.float32)
        own_sends(0, split_0, side, first[:, side * RIM : (side + 1) * RIM])

    @pl.when(jnp.logical_not(has_far))
    def _():
        for level in range(1, NSUB):
            rim[level - 1, FAR] = jnp.zeros((ROWS, RIM), jnp.float32)
        first_rim[FAR, 0:ROWS] = jnp.zeros((ROWS, RIM), jnp.float32)
        sums_in[...] = jnp.zeros((SUM_ROWS, RIM), jnp.float32)
        first_rim[FAR, ROWS:] = jnp.full((SPOT_ROWS, RIM), float(RIM), jnp.float32)

    pl.semaphore_wait(barrier, jnp.where(has_far, 4, 3))
    for side in SIDES:
        only_if_far(side, lambda: halo_copy(0, side).start())

    pl.semaphore_signal(two_on, inc=1, device_id=(tile, comp_at[3]), device_id_type=MESH)

    ghost_copies = [
        pltpu.make_async_remote_copy(
            src_ref=spec.at[pl.ds(at * NK, NK)],
            dst_ref=ghost.at[slot],
            send_sem=ghost_sent,
            recv_sem=ghost_recv,
            device_id=(tile, target),
            device_id_type=MESH,
        )
        for slot, at, target in ((0, DIRS - 1, comp_at[1]), (1, 0, comp_at[3]))
    ]

    def whole_rim(level, side):
        if level == 0:
            return first_rim[side, 0:ROWS]
        values = rim[level - 1, side]
        if (level, side) in ((1, FAR), (2, FAR), (2, NEAR), (3, FAR)):
            values = values + mended[side]
        return values

    def arrived(level, side):
        await_halo(level, side)
        return halves(whole_rim(level, side))

    def for_far(level, near):
        return pending_send[level % 2, FAR] + from_sends(near, NEAR_ROWS, FAR)

    def whole_list(level, side, both):
        return pending_send[level % 2, side] + from_sends(both, RIMS, side)

    def joined(near, far):
        return jnp.concatenate([near, far], axis=1)

    def next_points(both):
        return pending[...] + from_points(both, RIMS)

    near_0 = arrived(0, NEAR)
    send_halo(1, FAR, for_far(0, near_0))
    own_points(split_0, spec[...])
    await_bytes(misc, local_sem.at[5])
    sigma = wide(sigma_rim, PTS)
    angle = (lax.broadcasted_iota(jnp.int32, (8, PTS), 0) + comp * DIRS).astype(jnp.float32) * STEP
    aligned = jnp.cos(angle - misc[3:4])
    driven = misc[2:3] * sigma
    for d in range(DIRS):
        grown = 0.4 * jnp.maximum(driven * aligned[d : d + 1] - 0.3, 0.0)
        gain[d * NK : (d + 1) * NK] = wet * (1.0 + grown)
    far_0 = arrived(0, FAR)
    both_0 = joined(near_0, far_0)
    near_list_1 = whole_list(0, NEAR, both_0)
    far_list_1 = whole_list(0, FAR, both_0)
    points_1 = next_points(both_0)
    send_halo(1, NEAR, near_list_1)
    split_1 = halves(points_1)
    far_list_0 = first_out[FAR, 0:ROWS]
    own_sends(1, split_1, FAR, far_list_1)
    places = lax.broadcasted_iota(jnp.int32, (RIM, RIM), 0).astype(jnp.float32)
    for side in SIDES:
        for axis in range(2):
            spots = first_rim[side, ROWS + axis : ROWS + axis + 1]
            back_table[side, :, axis * RIM : (axis + 1) * RIM] = jnp.where(
                places == spots, 1.0, 0.0
            ).astype(jnp.bfloat16)
    mended[FAR] = mend(FAR, far_list_0)

    can_wait = lax.rem(tile, row_of_tiles) == row_of_tiles - 1

    def near_list_work():
        own_sends(1, split_1, NEAR, near_list_1)

    pl.when(jnp.logical_not(can_wait))(near_list_work)
    first_side = jnp.where(first_core, FAR, NEAR)

    def await_side(side):
        pl.when(jnp.logical_or(side == NEAR, has_far))(lambda: halo_copy(1, side).wait_recv())

    def send_past(side):
        other = 1 - side
        share = jnp.where(side == FAR, mended[FAR], 0.0)
        split = halves(rim[0, side] + share)
        rows_of_side = pl.ds(pl.multiple_of(PTS + RIM * side, RIM), RIM)
        outgoing[1, other] = pending_send[1, other] + weighed(
            gathered(split, send_table[other, rows_of_side])
        )
        pl.when(jnp.logical_or(other == NEAR, has_far))(lambda: halo_copy(2, other).start())

    await_side(first_side)
    send_past(first_side)
    await_side(1 - first_side)
    pl.when(jnp.logical_not(can_wait))(lambda: send_past(1 - first_side))
    near_1 = halves(whole_rim(1, NEAR))
    far_1 = halves(whole_rim(1, FAR))
    both_1 = joined(near_1, far_1)
    points_2 = wide(keep[...], PTS) * points_1 + from_points(joined(split_1, both_1), slice(0, EXT))
    far_list_2 = whole_list(1, FAR, both_1)
    split_2 = halves(points_2)
    own_sends(2, split_2, FAR, far_list_2)
    mended[NEAR] = mend(NEAR, near_list_1)

    def last_copy(first, past):
        inner = first > 0 and past < ROWS
        span = pl.ds(first, past - first)
        return pltpu.make_async_remote_copy(
            src_ref=outgoing.at[2, FAR, span],
            dst_ref=rim.at[2, FAR, span],
            send_sem=far_sent,
            recv_sem=last_recv.at[0] if inner else halo_recv.at[3, FAR],
            device_id=(far_tile, comp),
            device_id_type=MESH,
        )

    sums_copy = pltpu.make_async_remote_copy(
        src_ref=sums_out,
        dst_ref=sums_in,
        send_sem=last_sent,
        recv_sem=last_recv.at[1],
        device_id=(far_tile, comp),
        device_id_type=MESH,
    )
    near_2 = arrived(2, NEAR)
    far_sends = for_far(2, near_2)
    outgoing[2, FAR] = far_sends
    for first, past in ENDS:
        only_if_far(FAR, lambda: last_copy(first, past).start())
    sums_out[...] = upwind_sums(far_sends)
    only_if_far(FAR, lambda: sums_copy.start())
    for first, past in INNER:
        only_if_far(FAR, lambda: last_copy(first, past).start())

    @pl.when(can_wait)
    def _():
        near_list_work()
        send_halo(2, NEAR, pending_send[1, NEAR] + from_sends(far_1, FAR_ROWS, NEAR))

    mended[FAR] = mend(FAR, far_list_1)
    own_sends(2, split_2, NEAR, whole_list(1, NEAR, both_1))
    own_points(split_2, points_2)
    mended[LAST_FAR] = mend(FAR, far_list_2)
    mended_sums = upwind_sums(mended[LAST_FAR])
    both_2 = joined(near_2, arrived(2, FAR))
    send_halo(3, NEAR, whole_list(2, NEAR, both_2))
    points_3 = next_points(both_2)

    def chosen(values, spans):
        return jnp.concatenate([values[first:past] for first, past in spans], axis=0)

    def weighed_at(spans, picked):
        return (
            wide(chosen(across[...], spans), PTS) * picked[:, :PTS]
            + wide(chosen(along[...], spans), PTS) * picked[:, PTS:]
        )

    ends_picked, own_sums = gathered_both(
        chosen(points_3, ENDS), upwind_sums(points_3), table[OWN, :]
    )
    ends_own = wide(chosen(keep[...], ENDS), PTS) * chosen(points_3, ENDS) + weighed_at(
        ENDS, ends_picked
    )
    kept_sums = sums(points_3, keep)

    def rims_of(spans):
        near = [rim[2, NEAR, first:past] for first, past in spans]
        far = [
            rim[2, FAR, first:past] + mended[LAST_FAR, first:past] for first, past in spans
        ]
        return joined(jnp.concatenate(near, axis=0), jnp.concatenate(far, axis=0))

    await_halo(3, NEAR)

    @pl.when(has_far)
    def _():
        sums_copy.wait_recv()
        await_bytes(rim.at[2, FAR, pl.ds(0, 2 * NK)], halo_recv.at[3, FAR])

    turn = misc[0:1]
    moved = misc[1:2]
    rim_sums = jnp.concatenate([upwind_sums(rim[2, NEAR]), sums_in[...] + mended_sums], axis=1)
    ends_picked, rim_sums = gathered_both(rims_of(ENDS), rim_sums, table[RIMS, :])
    ends = ends_own + weighed_at(ENDS, ends_picked)
    upwind = own_sums + rim_sums
    across_sums = upwind[0 : SUM_ROWS // 2, :PTS]
    along_sums = upwind[SUM_ROWS // 2 :, PTS:]
    point_sums = [
        kept + across_sums[at : at + 1] + along_sums[at : at + 1]
        for at, kept in enumerate(kept_sums)
    ]

    def after_shift(still, up, down):
        return still - jnp.abs(moved) * (still - jnp.where(moved > 0, up, down))

    part[0:1] = after_shift(*point_sums[0:3])
    part[1:2] = after_shift(*point_sums[3:6])
    spec[0:NK] = ends[:NK]
    spec[ROWS - NK :] = ends[NK:]
    part_copies = [
        pltpu.make_async_remote_copy(
            src_ref=part,
            dst_ref=parts.at[hop - 1],
            send_sem=part_sent,
            recv_sem=part_recv,
            device_id=(tile, comp_at[hop]),
            device_id_type=MESH,
        )
        for hop in (2, 1, 3)
    ]
    pl.semaphore_wait(two_on, 1)
    for copy in part_copies + ghost_copies:
        copy.start()
    only_if_far(FAR, lambda: last_copy(*INNER[0]).wait_recv())
    inner = chosen(points_3, INNER)
    inner_picked = gathered(halves(joined(inner, rims_of(INNER))), table[...])
    spec[NK : ROWS - NK] = wide(chosen(keep[...], INNER), PTS) * inner + weighed_at(
        INNER, inner_picked
    )

    freq = lax.broadcasted_iota(jnp.int32, (NK, PTS), 0)

    def shifted(values):
        lower = jnp.where(freq == 0, 0.0, pltpu.roll(values, 1, 0))
        upper = jnp.where(freq == NK - 1, 0.0, pltpu.roll(values, NK - 1, 0))
        return values - jnp.abs(moved) * (values - jnp.where(moved > 0, lower, upper))

    def refracted(d):
        values = spec[d * NK : (d + 1) * NK]
        before = ghost[0] if d == 0 else spec[(d - 1) * NK : d * NK]
        beyond = ghost[1] if d == DIRS - 1 else spec[(d + 1) * NK : (d + 2) * NK]
        return values - jnp.abs(turn) * (values - jnp.where(turn > 0, before, beyond))

    def grown(d):
        return gain[d * NK : (d + 1) * NK] * shifted(refracted(d))

    for d in range(1, DIRS - 1):
        gain[d * NK : (d + 1) * NK] = grown(d)
    await_bytes(ghost, ghost_sent)
    await_bytes(parts, part_sent)
    halo_copy(0, NEAR).wait_send()
    await_bytes(outgoing.at[:, NEAR], near_sent)

    @pl.when(has_far)
    def _():
        halo_copy(0, FAR).wait_send()
        await_bytes(outgoing.at[:, FAR], far_sent)
        sums_copy.wait_send()

    await_bytes(parts, part_recv)
    whole = (part[...] + parts[0] + parts[1] + parts[2]) * jnp.float32(1.0 / COMPS)
    energy = whole[0:1]
    mean_freq = whole[1:2] / jnp.maximum(energy, 0.05)
    strength = mean_freq * mean_freq * mean_freq * energy * energy
    damping = 0.005 * (sigma * sigma) * strength
    factor = 1.0 / (1.0 + damping)
    for d in range(1, DIRS - 1):
        span = slice(d * NK, (d + 1) * NK)
        out_ref[span] = gain[span] * factor
    for first, past in ENDS:
        gain[first:past] = gain[first:past] * factor
    await_bytes(ghost, ghost_recv)
    for d in (0, DIRS - 1):
        out_ref[d * NK : (d + 1) * NK] = grown(d)


def shards(
    row_of_tiles,
    action,
    speed_courant,
    turning,
    freq_shift,
    wind_speed,
    wind_dir,
    sea_mask,
    neighbours,
    halo_rows,
):
    vmem = pltpu.VMEM
    f32 = jnp.float32
    dma = pltpu.SemaphoreType.DMA

    def row(values):
        return values.reshape(1, values.shape[0])

    return pl.pallas_call(
        functools.partial(kernel, row_of_tiles),
        out_shape=pltpu.VMEM((ROWS, PTS), f32),
        in_specs=[pl.BlockSpec(memory_space=pltpu.HBM)] * 9,
        out_specs=pl.BlockSpec(memory_space=pltpu.VMEM),
        scratch_shapes=[
            vmem((ROWS, PTS), f32),
            vmem((1, NK), f32),
            vmem((4, PTS), f32),
            vmem((1, PTS), jnp.int32),
            vmem((4, PTS), jnp.int32),
            vmem((1, 2 * RIM), jnp.int32),
            vmem((EXT, OWN_N), jnp.bfloat16),
            vmem((2, EXT, 2 * RIM), jnp.bfloat16),
            vmem((2, RIM, 2 * RIM), jnp.bfloat16),
            vmem((ROWS, RIM), f32),
            vmem((ROWS, RIM), f32),
            vmem((ROWS, RIM), f32),
            vmem((2, ROWS + SPOT_ROWS, RIM), f32),
            vmem((2, ROWS + SPOT_ROWS, RIM), f32),
            vmem((NSUB - 1, 2, ROWS, RIM), f32),
            vmem((NSUB - 1, 2, ROWS, RIM), f32),
            vmem((ROWS, PTS), f32),
            vmem((2, 2, ROWS, RIM), f32),
            vmem((3, ROWS, RIM), f32),
            vmem((ROWS, PTS), f32),
            vmem((2, NK, PTS), f32),
            vmem((2, PTS), f32),
            vmem((3, 2, PTS), f32),
            vmem((SUM_ROWS, RIM), f32),
            vmem((SUM_ROWS, RIM), f32),
            dma((6,)),
            dma((NSUB, 2)),
            dma,
            dma,
            dma,
            dma((2,)),
            pltpu.SemaphoreType.REGULAR,
        ],
        compiler_params=pltpu.CompilerParams(
            collective_id=0, has_side_effects=True, vmem_limit_bytes=48 * 1024 * 1024
        ),
        name="wave_step",
    )(
        *(
            pltpu.with_memory_space_constraint(values, pltpu.HBM)
            for values in (
                action,
                row(speed_courant),
                row(turning),
                row(freq_shift),
                row(wind_speed),
                row(wind_dir),
                row(sea_mask),
                neighbours,
                row(halo_rows),
            )
        )
    )


def solution(mesh):
    placed = (
        P("comp", "tiles"),
        P(),
        P("tiles"),
        P("tiles"),
        P("tiles"),
        P("tiles"),
        P("tiles"),
        P(None, "tiles"),
        P("tiles"),
    )
    return jax.shard_map(
        functools.partial(shards, mesh.shape["tiles"] // COMP_AXIS),
        mesh=mesh,
        in_specs=placed,
        out_specs=P("comp", "tiles"),
        check_vma=False,
    )
```

```python
import functools
import math

import jax
import jax.numpy as jnp
import numpy as np
from jax import lax
from jax.experimental import pallas as pl
from jax.experimental.pallas import tpu as pltpu
from jax.sharding import PartitionSpec as P

NSUB = 4
NTH = 24
NK = 32
PTS = 512
RIM = 128
EXT = PTS + 2 * RIM
COMP_AXIS = 4
DIRS = NTH // COMP_AXIS
ROWS = DIRS * NK
COMPS = NTH * NK
OWN_N = 2 * PTS
NEAR, FAR, LAST_FAR = 0, 1, 2
SPOT_ROWS = 8
SUM_ROWS = 16
ENDS = ((0, NK), (ROWS - NK, ROWS))
INNER = ((NK, ROWS - NK),)
MESH = pl.DeviceIdType.MESH
STEP = np.float32(2.0 * math.pi / NTH)
LOG_RATIO = np.float32(math.log(1.1))


def pick(index, values):
    chosen = jnp.float32(values[0])
    for place in range(1, len(values)):
        chosen = jnp.where(index == place, jnp.float32(values[place]), chosen)
    return chosen


def halves(values):
    high = values.astype(jnp.bfloat16)
    low = (values - high.astype(jnp.float32)).astype(jnp.bfloat16)
    return jnp.concatenate([high, low], axis=0)


def gathered(split, table):
    both = jnp.dot(split, table, preferred_element_type=jnp.float32)
    rows = both.shape[0] // 2
    return both[:rows] + both[rows:]


def gathered_both(first, second, table):
    split = jnp.concatenate([halves(first), halves(second)], axis=0)
    both = jnp.dot(split, table, preferred_element_type=jnp.float32)
    rows, more = (first.shape[0], second.shape[0])
    last = both[2 * rows :]
    return both[:rows] + both[rows : 2 * rows], last[:more] + last[more:]


def wide(column, lanes):
    return jnp.concatenate([column] * (lanes // RIM), axis=1)


def onehot(first, count, index):
    places = lax.broadcasted_iota(jnp.int32, (count, index.shape[1]), 0) + first
    return jnp.where(places == index, 1.0, 0.0).astype(jnp.bfloat16)


def kernel(
    row_of_tiles,
    action_hbm,
    speed_hbm,
    turning_hbm,
    shift_hbm,
    wind_hbm,
    dir_hbm,
    mask_hbm,
    links_hbm,
    rows_hbm,
    out_ref,
    spec,
    speed,
    misc,
    mask,
    links,
    rows,
    table,
    send_table,
    back_table,
    across,
    along,
    keep,
    first_out,
    first_rim,
    outgoing,
    rim,
    pending,
    pending_send,
    mended,
    gain,
    ghost,
    part,
    parts,
    sums_out,
    sums_in,
    local_sem,
    halo_recv,
    ghost_recv,
    part_recv,
    last_sent,
    last_recv,
    two_on,
):
    tile = lax.axis_index("tiles")
    comp = lax.axis_index("comp")
    tiles = lax.axis_size("tiles")
    first_core = lax.rem(tile, 2) == 0
    near_tile = jnp.where(first_core, tile + 1, tile - 1)
    far_tile = jnp.where(first_core, tile - 1, tile + 1)
    has_far = jnp.logical_and(far_tile >= 0, far_tile < tiles)
    far_tile = jnp.clip(far_tile, 0, tiles - 1)
    comp_at = [lax.rem(comp + step, COMP_AXIS) for step in range(COMP_AXIS)]

    barrier = pltpu.get_barrier_semaphore()

    @pl.when(has_far)
    def _():
        pl.semaphore_signal(barrier, inc=1, device_id=(far_tile, comp), device_id_type=MESH)

    for place in (
        (near_tile, comp),
        (tile, comp_at[1]),
        (tile, comp_at[3]),
    ):
        pl.semaphore_signal(barrier, inc=1, device_id=place, device_id_type=MESH)

    loads = [
        pltpu.make_async_copy(source, target, local_sem.at[number])
        for number, source, target in (
            (0, rows_hbm, rows),
            (1, mask_hbm, mask),
            (2, action_hbm, spec),
            (3, links_hbm, links),
            (4, speed_hbm, speed),
            (5, turning_hbm, misc.at[pl.ds(0, 1)]),
            (5, shift_hbm, misc.at[pl.ds(1, 1)]),
            (5, wind_hbm, misc.at[pl.ds(2, 1)]),
            (5, dir_hbm, misc.at[pl.ds(3, 1)]),
        )
    ]
    for load in loads:
        load.start()

    def await_bytes(ref, semaphore):
        pltpu.make_async_copy(ref, ref, semaphore).wait()

    near_sent, far_sent, ghost_sent, first_near_sent, first_far_sent, part_sent = (
        local_sem.at[number] for number in range(6)
    )

    def tile_at(side):
        if isinstance(side, int):
            return near_tile if side == NEAR else far_tile
        return jnp.where(side == NEAR, near_tile, far_tile)

    def halo_copy(level, side):
        if level == 0:
            source, target = (first_out.at[side], first_rim.at[side])
            sent = first_near_sent if side == NEAR else first_far_sent
        else:
            source, target = (outgoing.at[level - 1, side], rim.at[level - 1, side])
            sent = local_sem.at[side]
        return pltpu.make_async_remote_copy(
            src_ref=source,
            dst_ref=target,
            send_sem=sent,
            recv_sem=halo_recv.at[level, side],
            device_id=(tile_at(side), comp),
            device_id_type=MESH,
        )

    def only_if_far(side, action):
        if side == NEAR:
            action()
        else:
            pl.when(has_far)(action)

    def send_halo(level, side, values):
        outgoing[level - 1, side] = values
        only_if_far(side, lambda: halo_copy(level, side).start())

    def await_halo(level, side):
        only_if_far(side, lambda: halo_copy(level, side).wait_recv())

    OWN, NEAR_ROWS, FAR_ROWS = (slice(0, PTS), slice(PTS, PTS + RIM), slice(PTS + RIM, EXT))
    RIMS = slice(PTS, EXT)
    SIDES = (FAR, NEAR)

    loads[0].wait()
    low_rows, high_rows = (rows[:, 0:RIM], rows[:, RIM : 2 * RIM])
    near_rows = jnp.where(first_core, high_rows, low_rows)
    far_rows = jnp.where(first_core, low_rows, high_rows)
    picker = onehot(0, PTS, jnp.concatenate([near_rows, far_rows], axis=1))

    loads[1].wait()
    wet = mask[...].astype(jnp.float32)
    loads[3].wait()
    west_side = jnp.logical_or(comp == 0, comp == COMP_AXIS - 1)
    south_side = comp < 2
    near_first = jnp.where(first_core, RIM + PTS, 0)
    far_first = jnp.where(first_core, 0, RIM + PTS)
    for axis, index in enumerate(
        (
            jnp.where(west_side, links[0:1], links[1:2]),
            jnp.where(south_side, links[2:3], links[3:4]),
        )
    ):
        no_left = jnp.logical_and(tile == 0, index < RIM)
        no_right = jnp.logical_and(tile == tiles - 1, index >= RIM + PTS)
        nothing = jnp.logical_or(jnp.logical_or(no_left, no_right), mask[...] == 0)
        index = jnp.where(nothing, EXT, index)
        lanes = pl.ds(axis * PTS, PTS)
        table[0:PTS, lanes] = onehot(RIM, PTS, index)
        table[PTS : PTS + RIM, lanes] = onehot(near_first, RIM, index)
        table[PTS + RIM : EXT, lanes] = onehot(far_first, RIM, index)
    counted = lax.broadcasted_iota(jnp.int32, (RIM, RIM), 0).astype(jnp.float32)
    for axis in range(2):
        picked = jnp.dot(
            table[:, axis * PTS : (axis + 1) * PTS], picker, preferred_element_type=jnp.float32
        )
        for side in (NEAR, FAR):
            lanes = slice(RIM * axis, RIM * (axis + 1))
            chosen = picked[:, side * RIM : (side + 1) * RIM]
            send_table[side, :, lanes] = chosen.astype(jnp.bfloat16)
        for side, places in ((NEAR, NEAR_ROWS), (FAR, FAR_ROWS)):
            block = picked[places, side * RIM : (side + 1) * RIM]
            first_out[side, ROWS + axis : ROWS + axis + 1] = float(RIM) + jnp.sum(
                block * (counted - float(RIM)), axis=0, keepdims=True
            )

    loads[4].wait()
    diagonal = lax.broadcasted_iota(jnp.int32, (NK, NK), 0) == lax.broadcasted_iota(
        jnp.int32, (NK, NK), 1
    )
    courant = jnp.sum(jnp.where(diagonal, speed[...], 0.0), axis=1, keepdims=True)
    courant = jnp.broadcast_to(courant, (NK, RIM))
    angles = np.arange(NTH).astype(np.float32) * STEP
    cosines = np.abs(np.cos(angles)).reshape(COMP_AXIS, DIRS)
    sines = np.abs(np.sin(angles)).reshape(COMP_AXIS, DIRS)
    for d in range(DIRS):
        span = slice(d * NK, (d + 1) * NK)
        speed_x = courant * pick(comp, cosines[:, d])
        speed_y = courant * pick(comp, sines[:, d])
        across[span] = speed_x
        along[span] = speed_y
        keep[span] = 1.0 - speed_x - speed_y

    number = lax.broadcasted_iota(jnp.int32, (NK, RIM), 0)
    sigma_rim = jnp.exp((number - NK // 2).astype(jnp.float32) * LOG_RATIO)
    sigma_up = jnp.exp((number + 1 - NK // 2).astype(jnp.float32) * LOG_RATIO)
    sigma_down = jnp.exp((number - 1 - NK // 2).astype(jnp.float32) * LOG_RATIO)
    sigma_up = jnp.where(number == NK - 1, 0.0, sigma_up)
    sigma_down = jnp.where(number == 0, 0.0, sigma_down)
    weights = (
        sigma_rim,
        sigma_up,
        sigma_down,
        sigma_rim * sigma_rim,
        sigma_up * sigma_up,
        sigma_down * sigma_down,
    )

    def sums(values, shares):
        lanes = values.shape[1]
        total = wide(shares[0:NK], lanes) * values[0:NK]
        for d in range(1, DIRS):
            span = slice(d * NK, (d + 1) * NK)
            total = total + wide(shares[span], lanes) * values[span]
        return [
            jnp.sum(wide(weight, lanes) * total, axis=0, keepdims=True) for weight in weights
        ]

    def upwind_sums(values):
        gap = [jnp.zeros((SUM_ROWS // 2 - len(weights), values.shape[1]), jnp.float32)]
        return jnp.concatenate(sums(values, across) + gap + sums(values, along) + gap, axis=0)

    def weighed(picked):
        lanes = picked.shape[1] // 2
        return (
            wide(across[...], lanes) * picked[:, :lanes]
            + wide(along[...], lanes) * picked[:, lanes:]
        )

    def from_points(split, places):
        return weighed(gathered(split, table[places, :]))

    def from_sends(split, places, side):
        return weighed(gathered(split, send_table[side, places]))

    def own_points(split, values):
        pending[...] = wide(keep[...], PTS) * values + from_points(split, OWN)

    def own_sends(level, split, side, values):
        pending_send[level % 2, side] = keep[...] * values + from_sends(split, OWN, side)

    def mend(side, values):
        return weighed(gathered(halves(values), back_table[side]))

    loads[2].wait()
    spec[...] = spec[...] * wet
    split_0 = halves(spec[...])
    first = gathered(split_0, picker)
    for side in SIDES:
        first_out[side, 0:ROWS] = first[:, side * RIM : (side + 1) * RIM]
        first_out[side, ROWS + 2 :] = jnp.zeros((SPOT_ROWS - 2, RIM), jnp.float32)
        own_sends(0, split_0, side, first[:, side * RIM : (side + 1) * RIM])

    @pl.when(jnp.logical_not(has_far))
    def _():
        for level in range(1, NSUB):
            rim[level - 1, FAR] = jnp.zeros((ROWS, RIM), jnp.float32)
        first_rim[FAR, 0:ROWS] = jnp.zeros((ROWS, RIM), jnp.float32)
        sums_in[...] = jnp.zeros((SUM_ROWS, RIM), jnp.float32)
        first_rim[FAR, ROWS:] = jnp.full((SPOT_ROWS, RIM), float(RIM), jnp.float32)

    mended[FAR] = jnp.zeros((ROWS, RIM), jnp.float32)
    pl.semaphore_wait(barrier, jnp.where(has_far, 4, 3))
    for side in SIDES:
        only_if_far(side, lambda: halo_copy(0, side).start())

    pl.semaphore_signal(two_on, inc=1, device_id=(tile, comp_at[3]), device_id_type=MESH)

    ghost_copies = [
        pltpu.make_async_remote_copy(
            src_ref=spec.at[pl.ds(at * NK, NK)],
            dst_ref=ghost.at[slot],
            send_sem=ghost_sent,
            recv_sem=ghost_recv,
            device_id=(tile, target),
            device_id_type=MESH,
        )
        for slot, at, target in ((0, DIRS - 1, comp_at[1]), (1, 0, comp_at[3]))
    ]

    def whole_rim(level, side):
        if level == 0:
            return first_rim[side, 0:ROWS]
        values = rim[level - 1, side]
        if (level, side) in ((1, FAR), (2, FAR), (2, NEAR), (3, FAR)):
            values = values + mended[side]
        return values

    def arrived(level, side):
        await_halo(level, side)
        return halves(whole_rim(level, side))

    def for_far(level, near):
        return pending_send[level % 2, FAR] + from_sends(near, NEAR_ROWS, FAR)

    def whole_list(level, side, both):
        return pending_send[level % 2, side] + from_sends(both, RIMS, side)

    def joined(near, far):
        return jnp.concatenate([near, far], axis=1)

    def next_points(both):
        return pending[...] + from_points(both, RIMS)

    near_0 = arrived(0, NEAR)
    send_halo(1, FAR, for_far(0, near_0))
    own_points(split_0, spec[...])
    await_bytes(misc, local_sem.at[5])
    sigma = wide(sigma_rim, PTS)
    angle = (lax.broadcasted_iota(jnp.int32, (8, PTS), 0) + comp * DIRS).astype(jnp.float32) * STEP
    aligned = jnp.cos(angle - misc[3:4])
    driven = misc[2:3] * sigma
    for d in range(DIRS):
        grown = 0.4 * jnp.maximum(driven * aligned[d : d + 1] - 0.3, 0.0)
        gain[d * NK : (d + 1) * NK] = wet * (1.0 + grown)
    far_0 = arrived(0, FAR)
    both_0 = joined(near_0, far_0)
    near_list_1 = whole_list(0, NEAR, both_0)
    far_list_1 = whole_list(0, FAR, both_0)
    points_1 = next_points(both_0)
    send_halo(1, NEAR, near_list_1)
    split_1 = halves(points_1)
    own_sends(1, split_1, FAR, far_list_1)

    def far_share():
        places = lax.broadcasted_iota(jnp.int32, (RIM, RIM), 0).astype(jnp.float32)
        for side in SIDES:
            for axis in range(2):
                spots = first_rim[side, ROWS + axis : ROWS + axis + 1]
                back_table[side, :, axis * RIM : (axis + 1) * RIM] = jnp.where(
                    places == spots, 1.0, 0.0
                ).astype(jnp.bfloat16)
        mended[FAR] = mend(FAR, first_out[FAR, 0:ROWS])

    pl.when(first_core)(far_share)

    can_wait = lax.rem(tile, row_of_tiles) == row_of_tiles - 1

    def near_list_work():
        own_sends(1, split_1, NEAR, near_list_1)

    pl.when(jnp.logical_not(can_wait))(near_list_work)
    first_side = jnp.where(first_core, FAR, NEAR)

    def await_side(side):
        pl.when(jnp.logical_or(side == NEAR, has_far))(lambda: halo_copy(1, side).wait_recv())

    def send_past(side):
        other = 1 - side
        share = jnp.where(side == FAR, mended[FAR], 0.0)
        split = halves(rim[0, side] + share)
        rows_of_side = pl.ds(pl.multiple_of(PTS + RIM * side, RIM), RIM)
        outgoing[1, other] = pending_send[1, other] + weighed(
            gathered(split, send_table[other, rows_of_side])
        )
        pl.when(jnp.logical_or(other == NEAR, has_far))(lambda: halo_copy(2, other).start())

    await_side(first_side)
    send_past(first_side)
    pl.when(jnp.logical_not(first_core))(far_share)
    await_side(1 - first_side)
    pl.when(jnp.logical_not(can_wait))(lambda: send_past(1 - first_side))
    near_1 = halves(whole_rim(1, NEAR))
    far_1 = halves(whole_rim(1, FAR))
    both_1 = joined(near_1, far_1)
    points_2 = wide(keep[...], PTS) * points_1 + from_points(joined(split_1, both_1), slice(0, EXT))
    far_list_2 = whole_list(1, FAR, both_1)
    split_2 = halves(points_2)
    own_sends(2, split_2, FAR, far_list_2)
    mended[NEAR] = mend(NEAR, near_list_1)

    def last_copy(first, past):
        inner = first > 0 and past < ROWS
        span = pl.ds(first, past - first)
        return pltpu.make_async_remote_copy(
            src_ref=outgoing.at[2, FAR, span],
            dst_ref=rim.at[2, FAR, span],
            send_sem=far_sent,
            recv_sem=last_recv.at[0] if inner else halo_recv.at[3, FAR],
            device_id=(far_tile, comp),
            device_id_type=MESH,
        )

    sums_copy = pltpu.make_async_remote_copy(
        src_ref=sums_out,
        dst_ref=sums_in,
        send_sem=last_sent,
        recv_sem=last_recv.at[1],
        device_id=(far_tile, comp),
        device_id_type=MESH,
    )
    near_2 = arrived(2, NEAR)
    far_sends = for_far(2, near_2)
    outgoing[2, FAR] = far_sends
    for first, past in ENDS:
        only_if_far(FAR, lambda: last_copy(first, past).start())
    sums_out[...] = upwind_sums(far_sends)
    only_if_far(FAR, lambda: sums_copy.start())
    for first, past in INNER:
        only_if_far(FAR, lambda: last_copy(first, past).start())

    @pl.when(can_wait)
    def _():
        near_list_work()
        send_halo(2, NEAR, pending_send[1, NEAR] + from_sends(far_1, FAR_ROWS, NEAR))

    mended[FAR] = mend(FAR, far_list_1)
    own_sends(2, split_2, NEAR, whole_list(1, NEAR, both_1))
    own_points(split_2, points_2)
    mended[LAST_FAR] = mend(FAR, far_list_2)
    mended_sums = upwind_sums(mended[LAST_FAR])
    both_2 = joined(near_2, arrived(2, FAR))
    send_halo(3, NEAR, whole_list(2, NEAR, both_2))
    points_3 = next_points(both_2)

    def chosen(values, spans):
        return jnp.concatenate([values[first:past] for first, past in spans], axis=0)

    def weighed_at(spans, picked):
        return (
            wide(chosen(across[...], spans), PTS) * picked[:, :PTS]
            + wide(chosen(along[...], spans), PTS) * picked[:, PTS:]
        )

    ends_picked, own_sums = gathered_both(
        chosen(points_3, ENDS), upwind_sums(points_3), table[OWN, :]
    )
    ends_own = wide(chosen(keep[...], ENDS), PTS) * chosen(points_3, ENDS) + weighed_at(
        ENDS, ends_picked
    )
    kept_sums = sums(points_3, keep)

    def rims_of(spans):
        near = [rim[2, NEAR, first:past] for first, past in spans]
        far = [
            rim[2, FAR, first:past] + mended[LAST_FAR, first:past] for first, past in spans
        ]
        return joined(jnp.concatenate(near, axis=0), jnp.concatenate(far, axis=0))

    await_halo(3, NEAR)

    @pl.when(has_far)
    def _():
        sums_copy.wait_recv()
        await_bytes(rim.at[2, FAR, pl.ds(0, 2 * NK)], halo_recv.at[3, FAR])

    turn = misc[0:1]
    moved = misc[1:2]
    rim_sums = jnp.concatenate([upwind_sums(rim[2, NEAR]), sums_in[...] + mended_sums], axis=1)
    ends_picked, rim_sums = gathered_both(rims_of(ENDS), rim_sums, table[RIMS, :])
    ends = ends_own + weighed_at(ENDS, ends_picked)
    upwind = own_sums + rim_sums
    across_sums = upwind[0 : SUM_ROWS // 2, :PTS]
    along_sums = upwind[SUM_ROWS // 2 :, PTS:]
    point_sums = [
        kept + across_sums[at : at + 1] + along_sums[at : at + 1]
        for at, kept in enumerate(kept_sums)
    ]

    def after_shift(still, up, down):
        return still - jnp.abs(moved) * (still - jnp.where(moved > 0, up, down))

    part[0:1] = after_shift(*point_sums[0:3])
    part[1:2] = after_shift(*point_sums[3:6])
    spec[0:NK] = ends[:NK]
    spec[ROWS - NK :] = ends[NK:]
    part_copies = [
        pltpu.make_async_remote_copy(
            src_ref=part,
            dst_ref=parts.at[hop - 1],
            send_sem=part_sent,
            recv_sem=part_recv,
            device_id=(tile, comp_at[hop]),
            device_id_type=MESH,
        )
        for hop in (2, 1, 3)
    ]
    pl.semaphore_wait(two_on, 1)
    for copy in part_copies + ghost_copies:
        copy.start()
    only_if_far(FAR, lambda: last_copy(*INNER[0]).wait_recv())
    inner = chosen(points_3, INNER)
    inner_picked = gathered(halves(joined(inner, rims_of(INNER))), table[...])
    spec[NK : ROWS - NK] = wide(chosen(keep[...], INNER), PTS) * inner + weighed_at(
        INNER, inner_picked
    )

    freq = lax.broadcasted_iota(jnp.int32, (NK, PTS), 0)

    def shifted(values):
        lower = jnp.where(freq == 0, 0.0, pltpu.roll(values, 1, 0))
        upper = jnp.where(freq == NK - 1, 0.0, pltpu.roll(values, NK - 1, 0))
        return values - jnp.abs(moved) * (values - jnp.where(moved > 0, lower, upper))

    def refracted(d):
        values = spec[d * NK : (d + 1) * NK]
        before = ghost[0] if d == 0 else spec[(d - 1) * NK : d * NK]
        beyond = ghost[1] if d == DIRS - 1 else spec[(d + 1) * NK : (d + 2) * NK]
        return values - jnp.abs(turn) * (values - jnp.where(turn > 0, before, beyond))

    def grown(d):
        return gain[d * NK : (d + 1) * NK] * shifted(refracted(d))

    for d in range(1, DIRS - 1):
        gain[d * NK : (d + 1) * NK] = grown(d)
    await_bytes(ghost, ghost_sent)
    await_bytes(parts, part_sent)
    halo_copy(0, NEAR).wait_send()
    await_bytes(outgoing.at[:, NEAR], near_sent)

    @pl.when(has_far)
    def _():
        halo_copy(0, FAR).wait_send()
        await_bytes(outgoing.at[:, FAR], far_sent)
        sums_copy.wait_send()

    await_bytes(parts, part_recv)
    whole = (part[...] + parts[0] + parts[1] + parts[2]) * jnp.float32(1.0 / COMPS)
    energy = whole[0:1]
    mean_freq = whole[1:2] / jnp.maximum(energy, 0.05)
    strength = mean_freq * mean_freq * mean_freq * energy * energy
    damping = 0.005 * (sigma * sigma) * strength
    factor = 1.0 / (1.0 + damping)
    for d in range(1, DIRS - 1):
        span = slice(d * NK, (d + 1) * NK)
        out_ref[span] = gain[span] * factor
    for first, past in ENDS:
        gain[first:past] = gain[first:past] * factor
    await_bytes(ghost, ghost_recv)
    for d in (0, DIRS - 1):
        out_ref[d * NK : (d + 1) * NK] = grown(d)


def shards(
    row_of_tiles,
    action,
    speed_courant,
    turning,
    freq_shift,
    wind_speed,
    wind_dir,
    sea_mask,
    neighbours,
    halo_rows,
):
    vmem = pltpu.VMEM
    f32 = jnp.float32
    dma = pltpu.SemaphoreType.DMA

    def row(values):
        return values.reshape(1, values.shape[0])

    return pl.pallas_call(
        functools.partial(kernel, row_of_tiles),
        out_shape=pltpu.VMEM((ROWS, PTS), f32),
        in_specs=[pl.BlockSpec(memory_space=pltpu.HBM)] * 9,
        out_specs=pl.BlockSpec(memory_space=pltpu.VMEM),
        scratch_shapes=[
            vmem((ROWS, PTS), f32),
            vmem((1, NK), f32),
            vmem((4, PTS), f32),
            vmem((1, PTS), jnp.int32),
            vmem((4, PTS), jnp.int32),
            vmem((1, 2 * RIM), jnp.int32),
            vmem((EXT, OWN_N), jnp.bfloat16),
            vmem((2, EXT, 2 * RIM), jnp.bfloat16),
            vmem((2, RIM, 2 * RIM), jnp.bfloat16),
            vmem((ROWS, RIM), f32),
            vmem((ROWS, RIM), f32),
            vmem((ROWS, RIM), f32),
            vmem((2, ROWS + SPOT_ROWS, RIM), f32),
            vmem((2, ROWS + SPOT_ROWS, RIM), f32),
            vmem((NSUB - 1, 2, ROWS, RIM), f32),
            vmem((NSUB - 1, 2, ROWS, RIM), f32),
            vmem((ROWS, PTS), f32),
            vmem((2, 2, ROWS, RIM), f32),
            vmem((3, ROWS, RIM), f32),
            vmem((ROWS, PTS), f32),
            vmem((2, NK, PTS), f32),
            vmem((2, PTS), f32),
            vmem((3, 2, PTS), f32),
            vmem((SUM_ROWS, RIM), f32),
            vmem((SUM_ROWS, RIM), f32),
            dma((6,)),
            dma((NSUB, 2)),
            dma,
            dma,
            dma,
            dma((2,)),
            pltpu.SemaphoreType.REGULAR,
        ],
        compiler_params=pltpu.CompilerParams(
            collective_id=0, has_side_effects=True, vmem_limit_bytes=48 * 1024 * 1024
        ),
        name="wave_step",
    )(
        *(
            pltpu.with_memory_space_constraint(values, pltpu.HBM)
            for values in (
                action,
                row(speed_courant),
                row(turning),
                row(freq_shift),
                row(wind_speed),
                row(wind_dir),
                row(sea_mask),
                neighbours,
                row(halo_rows),
            )
        )
    )


def solution(mesh):
    placed = (
        P("comp", "tiles"),
        P(),
        P("tiles"),
        P("tiles"),
        P("tiles"),
        P("tiles"),
        P("tiles"),
        P(None, "tiles"),
        P("tiles"),
    )
    return jax.shard_map(
        functools.partial(shards, mesh.shape["tiles"] // COMP_AXIS),
        mesh=mesh,
        in_specs=placed,
        out_specs=P("comp", "tiles"),
        check_vma=False,
    )
```

```python
import functools
import math

import jax
import jax.numpy as jnp
import numpy as np
from jax import lax
from jax.experimental import pallas as pl
from jax.experimental.pallas import tpu as pltpu
from jax.sharding import PartitionSpec as P

NSUB = 4
NTH = 24
NK = 32
PTS = 512
RIM = 128
EXT = PTS + 2 * RIM
COMP_AXIS = 4
DIRS = NTH // COMP_AXIS
ROWS = DIRS * NK
COMPS = NTH * NK
OWN_N = 2 * PTS
NEAR, FAR, LAST_FAR = 0, 1, 2
SPOT_ROWS = 8
SUM_ROWS = 16
ENDS = ((0, NK), (ROWS - NK, ROWS))
INNER = ((NK, ROWS - NK),)
MESH = pl.DeviceIdType.MESH
STEP = np.float32(2.0 * math.pi / NTH)
LOG_RATIO = np.float32(math.log(1.1))


def pick(index, values):
    chosen = jnp.float32(values[0])
    for place in range(1, len(values)):
        chosen = jnp.where(index == place, jnp.float32(values[place]), chosen)
    return chosen


def halves(values):
    high = values.astype(jnp.bfloat16)
    low = (values - high.astype(jnp.float32)).astype(jnp.bfloat16)
    return jnp.concatenate([high, low], axis=0)


def gathered(split, table):
    both = jnp.dot(split, table, preferred_element_type=jnp.float32)
    rows = both.shape[0] // 2
    return both[:rows] + both[rows:]


def gathered_both(first, second, table):
    split = jnp.concatenate([halves(first), halves(second)], axis=0)
    both = jnp.dot(split, table, preferred_element_type=jnp.float32)
    rows, more = (first.shape[0], second.shape[0])
    last = both[2 * rows :]
    return both[:rows] + both[rows : 2 * rows], last[:more] + last[more:]


def wide(column, lanes):
    return jnp.concatenate([column] * (lanes // RIM), axis=1)


def onehot(first, count, index):
    places = lax.broadcasted_iota(jnp.int32, (count, index.shape[1]), 0) + first
    return jnp.where(places == index, 1.0, 0.0).astype(jnp.bfloat16)


def kernel(
    row_of_tiles,
    action_hbm,
    speed_hbm,
    turning_hbm,
    shift_hbm,
    wind_hbm,
    dir_hbm,
    mask_hbm,
    links_hbm,
    rows_hbm,
    out_ref,
    spec,
    speed,
    misc,
    mask,
    links,
    rows,
    table,
    send_table,
    back_table,
    across,
    along,
    keep,
    first_out,
    first_rim,
    outgoing,
    rim,
    pending,
    pending_send,
    mended,
    gain,
    ghost,
    part,
    parts,
    sums_out,
    sums_in,
    local_sem,
    halo_recv,
    ghost_recv,
    part_recv,
    last_recv,
    two_on,
):
    tile = lax.axis_index("tiles")
    comp = lax.axis_index("comp")
    tiles = lax.axis_size("tiles")
    first_core = lax.rem(tile, 2) == 0
    near_tile = jnp.where(first_core, tile + 1, tile - 1)
    far_tile = jnp.where(first_core, tile - 1, tile + 1)
    has_far = jnp.logical_and(far_tile >= 0, far_tile < tiles)
    far_tile = jnp.clip(far_tile, 0, tiles - 1)
    comp_at = [lax.rem(comp + step, COMP_AXIS) for step in range(COMP_AXIS)]

    barrier = pltpu.get_barrier_semaphore()

    @pl.when(has_far)
    def _():
        pl.semaphore_signal(barrier, inc=1, device_id=(far_tile, comp), device_id_type=MESH)

    for place in (
        (near_tile, comp),
        (tile, comp_at[1]),
        (tile, comp_at[3]),
    ):
        pl.semaphore_signal(barrier, inc=1, device_id=place, device_id_type=MESH)

    loads = [
        pltpu.make_async_copy(source, target, local_sem.at[number])
        for number, source, target in (
            (0, rows_hbm, rows),
            (1, mask_hbm, mask),
            (2, action_hbm, spec),
            (3, links_hbm, links),
            (4, speed_hbm, speed),
            (5, turning_hbm, misc.at[pl.ds(0, 1)]),
            (5, shift_hbm, misc.at[pl.ds(1, 1)]),
            (5, wind_hbm, misc.at[pl.ds(2, 1)]),
            (5, dir_hbm, misc.at[pl.ds(3, 1)]),
        )
    ]
    for load in loads:
        load.start()

    def await_bytes(ref, semaphore):
        pltpu.make_async_copy(ref, ref, semaphore).wait()

    near_sent, far_sent, ghost_sent, first_near_sent, first_far_sent, part_sent = (
        local_sem.at[number] for number in range(6)
    )

    def tile_at(side):
        if isinstance(side, int):
            return near_tile if side == NEAR else far_tile
        return jnp.where(side == NEAR, near_tile, far_tile)

    def halo_copy(level, side):
        if level == 0:
            source, target = (first_out.at[side], first_rim.at[side])
            sent = first_near_sent if side == NEAR else first_far_sent
        else:
            source, target = (outgoing.at[level - 1, side], rim.at[level - 1, side])
            sent = local_sem.at[side]
        return pltpu.make_async_remote_copy(
            src_ref=source,
            dst_ref=target,
            send_sem=sent,
            recv_sem=halo_recv.at[level, side],
            device_id=(tile_at(side), comp),
            device_id_type=MESH,
        )

    def only_if_far(side, action):
        if side == NEAR:
            action()
        else:
            pl.when(has_far)(action)

    def send_halo(level, side, values):
        outgoing[level - 1, side] = values
        only_if_far(side, lambda: halo_copy(level, side).start())

    def await_halo(level, side):
        only_if_far(side, lambda: halo_copy(level, side).wait_recv())

    OWN, NEAR_ROWS, FAR_ROWS = (slice(0, PTS), slice(PTS, PTS + RIM), slice(PTS + RIM, EXT))
    RIMS = slice(PTS, EXT)
    SIDES = (FAR, NEAR)

    loads[0].wait()
    low_rows, high_rows = (rows[:, 0:RIM], rows[:, RIM : 2 * RIM])
    near_rows = jnp.where(first_core, high_rows, low_rows)
    far_rows = jnp.where(first_core, low_rows, high_rows)
    picker = onehot(0, PTS, jnp.concatenate([near_rows, far_rows], axis=1))

    loads[1].wait()
    wet = mask[...].astype(jnp.float32)
    loads[3].wait()
    west_side = jnp.logical_or(comp == 0, comp == COMP_AXIS - 1)
    south_side = comp < 2
    near_first = jnp.where(first_core, RIM + PTS, 0)
    far_first = jnp.where(first_core, 0, RIM + PTS)
    for axis, index in enumerate(
        (
            jnp.where(west_side, links[0:1], links[1:2]),
            jnp.where(south_side, links[2:3], links[3:4]),
        )
    ):
        no_left = jnp.logical_and(tile == 0, index < RIM)
        no_right = jnp.logical_and(tile == tiles - 1, index >= RIM + PTS)
        nothing = jnp.logical_or(jnp.logical_or(no_left, no_right), mask[...] == 0)
        index = jnp.where(nothing, EXT, index)
        lanes = pl.ds(axis * PTS, PTS)
        table[0:PTS, lanes] = onehot(RIM, PTS, index)
        table[PTS : PTS + RIM, lanes] = onehot(near_first, RIM, index)
        table[PTS + RIM : EXT, lanes] = onehot(far_first, RIM, index)
    counted = lax.broadcasted_iota(jnp.int32, (RIM, RIM), 0).astype(jnp.float32)
    for axis in range(2):
        picked = jnp.dot(
            table[:, axis * PTS : (axis + 1) * PTS], picker, preferred_element_type=jnp.float32
        )
        for side in (NEAR, FAR):
            lanes = slice(RIM * axis, RIM * (axis + 1))
            chosen = picked[:, side * RIM : (side + 1) * RIM]
            send_table[side, :, lanes] = chosen.astype(jnp.bfloat16)
        for side, places in ((NEAR, NEAR_ROWS), (FAR, FAR_ROWS)):
            block = picked[places, side * RIM : (side + 1) * RIM]
            first_out[side, ROWS + axis : ROWS + axis + 1] = float(RIM) + jnp.sum(
                block * (counted - float(RIM)), axis=0, keepdims=True
            )

    loads[4].wait()
    diagonal = lax.broadcasted_iota(jnp.int32, (NK, NK), 0) == lax.broadcasted_iota(
        jnp.int32, (NK, NK), 1
    )
    courant = jnp.sum(jnp.where(diagonal, speed[...], 0.0), axis=1, keepdims=True)
    courant = jnp.broadcast_to(courant, (NK, RIM))
    angles = np.arange(NTH).astype(np.float32) * STEP
    cosines = np.abs(np.cos(angles)).reshape(COMP_AXIS, DIRS)
    sines = np.abs(np.sin(angles)).reshape(COMP_AXIS, DIRS)
    for d in range(DIRS):
        span = slice(d * NK, (d + 1) * NK)
        speed_x = courant * pick(comp, cosines[:, d])
        speed_y = courant * pick(comp, sines[:, d])
        across[span] = speed_x
        along[span] = speed_y
        keep[span] = 1.0 - speed_x - speed_y

    number = lax.broadcasted_iota(jnp.int32, (NK, RIM), 0)
    sigma_rim = jnp.exp((number - NK // 2).astype(jnp.float32) * LOG_RATIO)
    sigma_up = jnp.exp((number + 1 - NK // 2).astype(jnp.float32) * LOG_RATIO)
    sigma_down = jnp.exp((number - 1 - NK // 2).astype(jnp.float32) * LOG_RATIO)
    sigma_up = jnp.where(number == NK - 1, 0.0, sigma_up)
    sigma_down = jnp.where(number == 0, 0.0, sigma_down)
    weights = (
        sigma_rim,
        sigma_up,
        sigma_down,
        sigma_rim * sigma_rim,
        sigma_up * sigma_up,
        sigma_down * sigma_down,
    )

    def sums(values, shares):
        lanes = values.shape[1]
        total = wide(shares[0:NK], lanes) * values[0:NK]
        for d in range(1, DIRS):
            span = slice(d * NK, (d + 1) * NK)
            total = total + wide(shares[span], lanes) * values[span]
        return [
            jnp.sum(wide(weight, lanes) * total, axis=0, keepdims=True) for weight in weights
        ]

    def upwind_sums(values):
        gap = [jnp.zeros((SUM_ROWS // 2 - len(weights), values.shape[1]), jnp.float32)]
        return jnp.concatenate(sums(values, across) + gap + sums(values, along) + gap, axis=0)

    def weighed(picked):
        lanes = picked.shape[1] // 2
        return (
            wide(across[...], lanes) * picked[:, :lanes]
            + wide(along[...], lanes) * picked[:, lanes:]
        )

    def from_points(split, places):
        return weighed(gathered(split, table[places, :]))

    def from_sends(split, places, side):
        return weighed(gathered(split, send_table[side, places]))

    def own_points(split, values):
        pending[...] = wide(keep[...], PTS) * values + from_points(split, OWN)

    def own_sends(level, split, side, values):
        pending_send[level % 2, side] = keep[...] * values + from_sends(split, OWN, side)

    def mend(side, values):
        return weighed(gathered(halves(values), back_table[side]))

    loads[2].wait()
    spec[...] = spec[...] * wet
    split_0 = halves(spec[...])
    first = gathered(split_0, picker)
    for side in SIDES:
        first_out[side, 0:ROWS] = first[:, side * RIM : (side + 1) * RIM]
        first_out[side, ROWS + 2 :] = jnp.zeros((SPOT_ROWS - 2, RIM), jnp.float32)
        own_sends(0, split_0, side, first[:, side * RIM : (side + 1) * RIM])

    @pl.when(jnp.logical_not(has_far))
    def _():
        for level in range(1, NSUB):
            rim[level - 1, FAR] = jnp.zeros((ROWS, RIM), jnp.float32)
        first_rim[FAR, 0:ROWS] = jnp.zeros((ROWS, RIM), jnp.float32)
        sums_in[...] = jnp.zeros((SUM_ROWS, RIM), jnp.float32)
        first_rim[FAR, ROWS:] = jnp.full((SPOT_ROWS, RIM), float(RIM), jnp.float32)

    pl.semaphore_wait(barrier, jnp.where(has_far, 4, 3))
    for side in SIDES:
        only_if_far(side, lambda: halo_copy(0, side).start())

    pl.semaphore_signal(two_on, inc=1, device_id=(tile, comp_at[3]), device_id_type=MESH)

    ghost_copies = [
        pltpu.make_async_remote_copy(
            src_ref=spec.at[pl.ds(at * NK, NK)],
            dst_ref=ghost.at[slot],
            send_sem=ghost_sent,
            recv_sem=ghost_recv,
            device_id=(tile, target),
            device_id_type=MESH,
        )
        for slot, at, target in ((0, DIRS - 1, comp_at[1]), (1, 0, comp_at[3]))
    ]

    def whole_rim(level, side):
        if level == 0:
            return first_rim[side, 0:ROWS]
        values = rim[level - 1, side]
        if (level, side) in ((1, FAR), (2, FAR), (2, NEAR), (3, FAR)):
            values = values + mended[side]
        return values

    def arrived(level, side):
        await_halo(level, side)
        return halves(whole_rim(level, side))

    def for_far(level, near):
        return pending_send[level % 2, FAR] + from_sends(near, NEAR_ROWS, FAR)

    def whole_list(level, side, both):
        return pending_send[level % 2, side] + from_sends(both, RIMS, side)

    def joined(near, far):
        return jnp.concatenate([near, far], axis=1)

    def next_points(both):
        return pending[...] + from_points(both, RIMS)

    near_0 = arrived(0, NEAR)
    send_halo(1, FAR, for_far(0, near_0))
    own_points(split_0, spec[...])
    await_bytes(misc, local_sem.at[5])
    sigma = wide(sigma_rim, PTS)
    angle = (lax.broadcasted_iota(jnp.int32, (8, PTS), 0) + comp * DIRS).astype(jnp.float32) * STEP
    aligned = jnp.cos(angle - misc[3:4])
    driven = misc[2:3] * sigma
    for d in range(DIRS):
        grown = 0.4 * jnp.maximum(driven * aligned[d : d + 1] - 0.3, 0.0)
        gain[d * NK : (d + 1) * NK] = wet * (1.0 + grown)
    far_0 = arrived(0, FAR)
    both_0 = joined(near_0, far_0)
    near_list_1 = whole_list(0, NEAR, both_0)
    far_list_1 = whole_list(0, FAR, both_0)
    points_1 = next_points(both_0)
    send_halo(1, NEAR, near_list_1)
    split_1 = halves(points_1)
    far_list_0 = first_out[FAR, 0:ROWS]
    own_sends(1, split_1, FAR, far_list_1)
    places = lax.broadcasted_iota(jnp.int32, (RIM, RIM), 0).astype(jnp.float32)
    for side in SIDES:
        for axis in range(2):
            spots = first_rim[side, ROWS + axis : ROWS + axis + 1]
            back_table[side, :, axis * RIM : (axis + 1) * RIM] = jnp.where(
                places == spots, 1.0, 0.0
            ).astype(jnp.bfloat16)
    mended[FAR] = mend(FAR, far_list_0)

    can_wait = lax.rem(tile, row_of_tiles) == row_of_tiles - 1

    def near_list_work():
        own_sends(1, split_1, NEAR, near_list_1)

    pl.when(jnp.logical_not(can_wait))(near_list_work)
    first_side = jnp.where(first_core, FAR, NEAR)

    def await_side(side):
        pl.when(jnp.logical_or(side == NEAR, has_far))(lambda: halo_copy(1, side).wait_recv())

    def send_past(side):
        other = 1 - side
        share = jnp.where(side == FAR, mended[FAR], 0.0)
        split = halves(rim[0, side] + share)
        rows_of_side = pl.ds(pl.multiple_of(PTS + RIM * side, RIM), RIM)
        outgoing[1, other] = pending_send[1, other] + weighed(
            gathered(split, send_table[other, rows_of_side])
        )
        pl.when(jnp.logical_or(other == NEAR, has_far))(lambda: halo_copy(2, other).start())

    await_side(first_side)
    send_past(first_side)
    await_side(1 - first_side)
    pl.when(jnp.logical_not(can_wait))(lambda: send_past(1 - first_side))
    near_1 = halves(whole_rim(1, NEAR))
    far_1 = halves(whole_rim(1, FAR))
    both_1 = joined(near_1, far_1)
    points_2 = wide(keep[...], PTS) * points_1 + from_points(joined(split_1, both_1), slice(0, EXT))
    far_list_2 = whole_list(1, FAR, both_1)
    split_2 = halves(points_2)
    own_sends(2, split_2, FAR, far_list_2)
    mended[NEAR] = mend(NEAR, near_list_1)

    def last_copy(first, past):
        inner = first > 0 and past < ROWS
        span = pl.ds(first, past - first)
        return pltpu.make_async_remote_copy(
            src_ref=outgoing.at[2, FAR, span],
            dst_ref=rim.at[2, FAR, span],
            send_sem=far_sent,
            recv_sem=last_recv.at[0] if inner else halo_recv.at[3, FAR],
            device_id=(far_tile, comp),
            device_id_type=MESH,
        )

    sums_copy = pltpu.make_async_remote_copy(
        src_ref=sums_out,
        dst_ref=sums_in,
        send_sem=first_near_sent,
        recv_sem=last_recv.at[1],
        device_id=(far_tile, comp),
        device_id_type=MESH,
    )
    near_2 = arrived(2, NEAR)
    far_sends = for_far(2, near_2)
    outgoing[2, FAR] = far_sends
    for first, past in ENDS:
        only_if_far(FAR, lambda: last_copy(first, past).start())
    halo_copy(0, NEAR).wait_send()
    sums_out[...] = upwind_sums(far_sends)
    only_if_far(FAR, lambda: sums_copy.start())
    for first, past in INNER:
        only_if_far(FAR, lambda: last_copy(first, past).start())

    @pl.when(can_wait)
    def _():
        near_list_work()
        send_halo(2, NEAR, pending_send[1, NEAR] + from_sends(far_1, FAR_ROWS, NEAR))

    mended[FAR] = mend(FAR, far_list_1)
    own_sends(2, split_2, NEAR, whole_list(1, NEAR, both_1))
    own_points(split_2, points_2)
    mended[LAST_FAR] = mend(FAR, far_list_2)
    mended_sums = upwind_sums(mended[LAST_FAR])
    both_2 = joined(near_2, arrived(2, FAR))
    send_halo(3, NEAR, whole_list(2, NEAR, both_2))
    points_3 = next_points(both_2)

    def chosen(values, spans):
        return jnp.concatenate([values[first:past] for first, past in spans], axis=0)

    def weighed_at(spans, picked):
        return (
            wide(chosen(across[...], spans), PTS) * picked[:, :PTS]
            + wide(chosen(along[...], spans), PTS) * picked[:, PTS:]
        )

    ends_picked, own_sums = gathered_both(
        chosen(points_3, ENDS), upwind_sums(points_3), table[OWN, :]
    )
    ends_own = wide(chosen(keep[...], ENDS), PTS) * chosen(points_3, ENDS) + weighed_at(
        ENDS, ends_picked
    )
    kept_sums = sums(points_3, keep)

    def rims_of(spans):
        near = [rim[2, NEAR, first:past] for first, past in spans]
        far = [
            rim[2, FAR, first:past] + mended[LAST_FAR, first:past] for first, past in spans
        ]
        return joined(jnp.concatenate(near, axis=0), jnp.concatenate(far, axis=0))

    await_halo(3, NEAR)

    @pl.when(has_far)
    def _():
        sums_copy.wait_recv()
        await_bytes(rim.at[2, FAR, pl.ds(0, 2 * NK)], halo_recv.at[3, FAR])

    turn = misc[0:1]
    moved = misc[1:2]
    rim_sums = jnp.concatenate([upwind_sums(rim[2, NEAR]), sums_in[...] + mended_sums], axis=1)
    ends_picked, rim_sums = gathered_both(rims_of(ENDS), rim_sums, table[RIMS, :])
    ends = ends_own + weighed_at(ENDS, ends_picked)
    upwind = own_sums + rim_sums
    across_sums = upwind[0 : SUM_ROWS // 2, :PTS]
    along_sums = upwind[SUM_ROWS // 2 :, PTS:]
    point_sums = [
        kept + across_sums[at : at + 1] + along_sums[at : at + 1]
        for at, kept in enumerate(kept_sums)
    ]

    def after_shift(still, up, down):
        return still - jnp.abs(moved) * (still - jnp.where(moved > 0, up, down))

    part[0:1] = after_shift(*point_sums[0:3])
    part[1:2] = after_shift(*point_sums[3:6])
    spec[0:NK] = ends[:NK]
    spec[ROWS - NK :] = ends[NK:]
    part_copies = [
        pltpu.make_async_remote_copy(
            src_ref=part,
            dst_ref=parts.at[hop - 1],
            send_sem=part_sent,
            recv_sem=part_recv,
            device_id=(tile, comp_at[hop]),
            device_id_type=MESH,
        )
        for hop in (2, 1, 3)
    ]
    pl.semaphore_wait(two_on, 1)
    for copy in part_copies + ghost_copies:
        copy.start()
    only_if_far(FAR, lambda: last_copy(*INNER[0]).wait_recv())
    inner = chosen(points_3, INNER)
    inner_picked = gathered(halves(joined(inner, rims_of(INNER))), table[...])
    spec[NK : ROWS - NK] = wide(chosen(keep[...], INNER), PTS) * inner + weighed_at(
        INNER, inner_picked
    )

    freq = lax.broadcasted_iota(jnp.int32, (NK, PTS), 0)

    def shifted(values):
        lower = jnp.where(freq == 0, 0.0, pltpu.roll(values, 1, 0))
        upper = jnp.where(freq == NK - 1, 0.0, pltpu.roll(values, NK - 1, 0))
        return values - jnp.abs(moved) * (values - jnp.where(moved > 0, lower, upper))

    def refracted(d):
        values = spec[d * NK : (d + 1) * NK]
        before = ghost[0] if d == 0 else spec[(d - 1) * NK : d * NK]
        beyond = ghost[1] if d == DIRS - 1 else spec[(d + 1) * NK : (d + 2) * NK]
        return values - jnp.abs(turn) * (values - jnp.where(turn > 0, before, beyond))

    def grown(d):
        return gain[d * NK : (d + 1) * NK] * shifted(refracted(d))

    for d in range(1, DIRS - 1):
        gain[d * NK : (d + 1) * NK] = grown(d)
    await_bytes(ghost, ghost_sent)
    await_bytes(parts, part_sent)
    await_bytes(outgoing.at[:, NEAR], near_sent)

    @pl.when(has_far)
    def _():
        halo_copy(0, FAR).wait_send()
        await_bytes(outgoing.at[:, FAR], far_sent)
        sums_copy.wait_send()

    await_bytes(parts, part_recv)
    whole = (part[...] + parts[0] + parts[1] + parts[2]) * jnp.float32(1.0 / COMPS)
    energy = whole[0:1]
    mean_freq = whole[1:2] / jnp.maximum(energy, 0.05)
    strength = mean_freq * mean_freq * mean_freq * energy * energy
    damping = 0.005 * (sigma * sigma) * strength
    factor = 1.0 / (1.0 + damping)
    for d in range(1, DIRS - 1):
        span = slice(d * NK, (d + 1) * NK)
        out_ref[span] = gain[span] * factor
    for first, past in ENDS:
        gain[first:past] = gain[first:past] * factor
    await_bytes(ghost, ghost_recv)
    for d in (0, DIRS - 1):
        out_ref[d * NK : (d + 1) * NK] = grown(d)


def shards(
    row_of_tiles,
    action,
    speed_courant,
    turning,
    freq_shift,
    wind_speed,
    wind_dir,
    sea_mask,
    neighbours,
    halo_rows,
):
    vmem = pltpu.VMEM
    f32 = jnp.float32
    dma = pltpu.SemaphoreType.DMA

    def row(values):
        return values.reshape(1, values.shape[0])

    return pl.pallas_call(
        functools.partial(kernel, row_of_tiles),
        out_shape=pltpu.VMEM((ROWS, PTS), f32),
        in_specs=[pl.BlockSpec(memory_space=pltpu.HBM)] * 9,
        out_specs=pl.BlockSpec(memory_space=pltpu.VMEM),
        scratch_shapes=[
            vmem((ROWS, PTS), f32),
            vmem((1, NK), f32),
            vmem((4, PTS), f32),
            vmem((1, PTS), jnp.int32),
            vmem((4, PTS), jnp.int32),
            vmem((1, 2 * RIM), jnp.int32),
            vmem((EXT, OWN_N), jnp.bfloat16),
            vmem((2, EXT, 2 * RIM), jnp.bfloat16),
            vmem((2, RIM, 2 * RIM), jnp.bfloat16),
            vmem((ROWS, RIM), f32),
            vmem((ROWS, RIM), f32),
            vmem((ROWS, RIM), f32),
            vmem((2, ROWS + SPOT_ROWS, RIM), f32),
            vmem((2, ROWS + SPOT_ROWS, RIM), f32),
            vmem((NSUB - 1, 2, ROWS, RIM), f32),
            vmem((NSUB - 1, 2, ROWS, RIM), f32),
            vmem((ROWS, PTS), f32),
            vmem((2, 2, ROWS, RIM), f32),
            vmem((3, ROWS, RIM), f32),
            vmem((ROWS, PTS), f32),
            vmem((2, NK, PTS), f32),
            vmem((2, PTS), f32),
            vmem((3, 2, PTS), f32),
            vmem((SUM_ROWS, RIM), f32),
            vmem((SUM_ROWS, RIM), f32),
            dma((6,)),
            dma((NSUB, 2)),
            dma,
            dma,
            dma((2,)),
            pltpu.SemaphoreType.REGULAR,
        ],
        compiler_params=pltpu.CompilerParams(
            collective_id=0, has_side_effects=True, vmem_limit_bytes=48 * 1024 * 1024
        ),
        name="wave_step",
    )(
        *(
            pltpu.with_memory_space_constraint(values, pltpu.HBM)
            for values in (
                action,
                row(speed_courant),
                row(turning),
                row(freq_shift),
                row(wind_speed),
                row(wind_dir),
                row(sea_mask),
                neighbours,
                row(halo_rows),
            )
        )
    )


def solution(mesh):
    placed = (
        P("comp", "tiles"),
        P(),
        P("tiles"),
        P("tiles"),
        P("tiles"),
        P("tiles"),
        P("tiles"),
        P(None, "tiles"),
        P("tiles"),
    )
    return jax.shard_map(
        functools.partial(shards, mesh.shape["tiles"] // COMP_AXIS),
        mesh=mesh,
        in_specs=placed,
        out_specs=P("comp", "tiles"),
        check_vma=False,
    )
```
